256 devices in a mesh: frag: 8 (over y, core), band: 32 (over x, z).
Axes of the slice: x: 4, y: 4, z: 8, core: 2. Of those that a mesh axis runs over, the one named last changes fastest.
Arguments:
- wave_coeffs: bfloat16 [8, 256, 262144], P('frag', 'band'), may hold values from -40 to 40
- old_potential: float32 [8, 262144], P('frag'), may hold values from -4 to 4
- occupations: float32 [8, 256], P('frag'), may hold values from 0 to 2
- box_sizes: int32 [8, 3], replicated, may hold values from 32 to 64, as said below
- box_offsets: int32 [8, 3], replicated, may hold values from 0 to 96, as said below
- patch_signs: int32 [8], replicated, may hold values from -1 to 1, as said below
Outputs:
- new_waves: bfloat16 [8, 256, 262144], P('frag', 'band')
- box_potential: float32 [8, 262144], P('frag')
- total_potential: float32 [128, 128, 128], P('band')
The draws below stay inside these ranges and needn't reach their ends.
Inputs may be any that keep to these rules, and one draw needn't show every extreme that they name: `box_sizes`: each entry is 32, 48 or 64. box_offsets + box_sizes <= 128 in every dimension. `patch_signs`: each entry is -1 or 1.
All inputs are finite; a program needn't handle non-finite values.
Results may differ from the reference program's by a relative error of at most 0.0065.
Values may be sent and summed in bfloat16 or wider, within the bound.
No kernel may reach another device: no remote copies, remote signals or barrier semaphores. Data moves between devices by JAX's collectives and lax.ppermute only.
A program may use at most 192 MiB of HBM per device.

```python
import jax
import jax.numpy as jnp
from jax import lax

NB = 256
BOX = 64
G = 128
NS_ITERS = 8
FRAGS = 8
N_BAND = 32


def box_layout(key):
    size_key = jax.random.fold_in(key, 11)
    offset_key = jax.random.fold_in(key, 12)
    levels = jax.random.randint(size_key, (FRAGS, 3), 0, 3)
    levels = levels.at[0, :].set(2)
    levels = levels.at[1, :].set(0)
    levels = levels.at[2, 0].set(0)
    box_sizes = BOX // 4 * (2 + levels)
    raw_offsets = jax.random.randint(offset_key, (FRAGS, 3), 0, G - BOX // 2 + 1)
    offsets = raw_offsets % (G - box_sizes + 1)
    offsets = offsets.at[0, 0].set(0)
    offsets = offsets.at[1, 0].set(G - BOX // 2)
    offsets = offsets.at[2, 0].set(G // N_BAND)
    return (box_sizes.astype(jnp.int32), offsets.astype(jnp.int32))


def draw_box_sizes(key, part):
    return box_layout(key)[0]


def draw_box_offsets(key, part):
    return box_layout(key)[1]


def draw_patch_signs(key, part):
    signs = 2 * jax.random.randint(jax.random.fold_in(key, 21), (FRAGS,), 0, 2) - 1
    signs = signs.at[0].set(1)
    signs = signs.at[1].set(-1)
    return signs.astype(jnp.int32)


def draw_wave_coeffs(key, part):
    scale_key = jax.random.fold_in(key, 31)
    value_key = jax.random.fold_in(key, 32)
    scales = jnp.exp(jax.random.uniform(scale_key, (FRAGS, NB, 1), jnp.float32, 0.0, jnp.log(10.0)))
    values = scales * jnp.clip(jax.random.normal(value_key, (FRAGS, NB, BOX ** 3), jnp.float32), -4.0, 4.0)
    return values.astype(jnp.bfloat16)


def level_of(own_key, extent, shards, least, largest):
    factor_of = 1.0
    for axis_at, blocks in shards:
        heights = jax.random.uniform(jax.random.fold_in(jax.random.fold_in(own_key, 6), axis_at), (blocks,), jnp.float32, least / len(shards), largest / len(shards))
        factor_of = factor_of * jnp.repeat(jnp.exp(heights), extent[axis_at] // blocks).reshape((-1,) + (1,) * (len(extent) - 1 - axis_at))
    return factor_of


def noise(own_key, shape, deviation, reach, shards=(), kind=jnp.bfloat16):
    entries = deviation * jax.random.normal(own_key, shape, jnp.float32)
    if shards:
        entries = entries * level_of(own_key, shape, shards, -0.22, 0.18)
    return jnp.clip(entries, -reach, reach).astype(kind)


def setup_inputs(seed: int = 0) -> dict:
    seeds = jax.random.split(jax.random.key(seed), 7)
    wave_coeffs = draw_wave_coeffs(jax.random.fold_in(seeds[6], 71), 0)
    old_potential = noise(seeds[1], (FRAGS, BOX**3), 1.0, 4.0, ((0, 8),), jnp.float32)
    occupations = jnp.clip(2.0 * jax.random.uniform(seeds[2], (FRAGS, NB), jnp.float32) ** level_of(seeds[2], (FRAGS, NB), ((0, 8),), -0.2, 0.2), 0.0, 2.0)
    box_sizes = draw_box_sizes(jax.random.fold_in(seeds[6], 71), 0)
    box_offsets = draw_box_offsets(jax.random.fold_in(seeds[6], 71), 0)
    patch_signs = draw_patch_signs(jax.random.fold_in(seeds[6], 71), 0)
    return {"wave_coeffs": wave_coeffs, "old_potential": old_potential, "occupations": occupations, "box_sizes": box_sizes, "box_offsets": box_offsets, "patch_signs": patch_signs}


step_size = 0.1
screening = 0.5
local_factor = 0.75
epsilon = 1e-06

def box_mask(box_size):
    coords = jnp.arange(BOX).astype(jnp.int32)
    along_x = (coords < box_size[0]).astype(jnp.float32)
    along_y = (coords < box_size[1]).astype(jnp.float32)
    along_z = (coords < box_size[2]).astype(jnp.float32)
    return (along_x[:, None, None] * along_y[None, :, None] * along_z[None, None, :]).reshape(BOX * BOX * BOX)

def sine_table():
    index = jnp.arange(G).astype(jnp.float32) + 1.0
    table = jnp.sqrt(2.0 / (G + 1)) * jnp.sin(jnp.pi * index[:, None] * index[None, :] / (G + 1))
    eigen = 2.0 - 2.0 * jnp.cos(jnp.pi * index / (G + 1))
    return (table, eigen)

def newton_schulz(gram):
    highest = lax.Precision.HIGHEST
    frobenius = jnp.sqrt(jnp.sum(gram * gram) + epsilon)
    identity = jnp.eye(NB, dtype=jnp.float32)
    square_part = gram / frobenius
    inverse_part = identity
    for sweep in range(NS_ITERS):
        newton_step = 0.5 * (3.0 * identity - jnp.dot(inverse_part, square_part, precision=highest, preferred_element_type=jnp.float32))
        square_part = jnp.dot(square_part, newton_step, precision=highest, preferred_element_type=jnp.float32)
        inverse_part = jnp.dot(newton_step, inverse_part, precision=highest, preferred_element_type=jnp.float32)
    return (inverse_part / jnp.sqrt(frobenius)).astype(jnp.bfloat16)

def reference(wave_coeffs, old_potential, occupations, box_sizes, box_offsets, patch_signs):
    highest = lax.Precision.HIGHEST
    cell_volume = 1.0 / BOX ** 3
    table, eigen = sine_table()
    fresh_list = []
    patched = jnp.zeros((G, G, G), jnp.float32)
    for fragment in range(FRAGS):
        mask = box_mask(box_sizes[fragment])
        waves = wave_coeffs[fragment].astype(jnp.float32) * mask[None, :]
        cube = waves.reshape(NB, BOX, BOX, BOX)
        padded = jnp.pad(cube, ((0, 0), (1, 1), (1, 1), (1, 1)))
        beside = padded[:, 2:, 1:-1, 1:-1] + padded[:, :-2, 1:-1, 1:-1]
        beside = beside + padded[:, 1:-1, 2:, 1:-1] + padded[:, 1:-1, :-2, 1:-1]
        beside = beside + padded[:, 1:-1, 1:-1, 2:] + padded[:, 1:-1, 1:-1, :-2]
        kinetic = (6.0 * cube - beside).reshape(NB, BOX * BOX * BOX)
        applied = 0.5 * kinetic + old_potential[fragment][None, :] * waves
        trial = (mask[None, :] * (waves - step_size * applied)).astype(jnp.bfloat16)
        gram = lax.dot_general(trial, trial, (((1,), (1,)), ((), ())), preferred_element_type=jnp.float32) * cell_volume
        coeff = newton_schulz(gram)
        fresh = lax.dot_general(coeff, trial, (((0,), (0,)), ((), ())), preferred_element_type=jnp.float32)
        fresh_list.append(fresh.astype(jnp.bfloat16))
        density = lax.optimization_barrier(jnp.sum(occupations[fragment][:, None] * fresh * fresh, axis=0)) / NB
        frame = jnp.zeros((G + BOX, G + BOX, G + BOX), jnp.float32)
        start = box_offsets[fragment].astype(jnp.int32)
        frame = lax.dynamic_update_slice(frame, density.reshape(BOX, BOX, BOX), (start[0], start[1], start[2]))
        patched = patched + patch_signs[fragment].astype(jnp.float32) * frame[:G, :G, :G]
    spectrum = jnp.einsum('abc,ci->abi', patched, table, precision=highest)
    spectrum = jnp.einsum('abc,bi->aic', spectrum, table, precision=highest)
    spectrum = jnp.einsum('abc,ai->ibc', spectrum, table, precision=highest)
    spectrum = spectrum * (screening / (eigen[:, None, None] + eigen[None, :, None] + eigen[None, None, :] + screening))
    spectrum = jnp.einsum('abc,ai->ibc', spectrum, table, precision=highest)
    spectrum = jnp.einsum('abc,bi->aic', spectrum, table, precision=highest)
    hartree = jnp.einsum('abc,ci->abi', spectrum, table, precision=highest)
    total_potential = hartree - local_factor * jnp.cbrt(jnp.maximum(patched, 0.0))
    extended = jnp.pad(total_potential, ((0, BOX), (0, BOX), (0, BOX)))
    windows = []
    for fragment in range(FRAGS):
        mask = box_mask(box_sizes[fragment])
        start = box_offsets[fragment].astype(jnp.int32)
        window = lax.dynamic_slice(extended, (start[0], start[1], start[2]), (BOX, BOX, BOX))
        windows.append(window.reshape(BOX * BOX * BOX) * mask)
    return (jnp.stack(fresh_list), jnp.stack(windows), total_potential)
```

```python
import functools

import jax
import jax.numpy as jnp
import numpy as np
from jax import lax
from jax.experimental import pallas as pl
from jax.experimental.pallas import tpu as pltpu
from jax.sharding import PartitionSpec as P

NB = 256
BOX = 64
G = 128
NS_ITERS = 8
CELLS = BOX**3
PLANE = BOX * BOX
PEERS = 32
OWN = NB // PEERS
FULL = CELLS // PEERS
EXTRA = FULL // OWN
STRIDE = PLANE + 128
ROWS = PLANE // 128
VOLUMES = (8, 12, 16, 18, 24, 27, 32, 36, 48, 64)

step_size = 0.1
screening = 0.5
local_factor = 0.75
epsilon = 1e-06
HIGHEST = lax.Precision.HIGHEST
f32 = jnp.float32
bf16 = jnp.bfloat16


def sine_table():
    index = np.arange(G, dtype=np.float64) + 1.0
    table = np.sqrt(2.0 / (G + 1)) * np.sin(np.pi * index[:, None] * index[None, :] / (G + 1))
    eigen = 2.0 - 2.0 * np.cos(np.pi * index / (G + 1))
    padded = np.zeros((G + BOX, G), np.float32)
    padded[:G] = table
    return padded, eigen.astype(np.float32)


def aligned(offset):
    return pl.multiple_of(offset, 128)


def vmem():
    return pl.BlockSpec(memory_space=pltpu.VMEM)


def smem():
    return pl.BlockSpec(memory_space=pltpu.SMEM)


def params(mib):
    return pltpu.CompilerParams(vmem_limit_bytes=mib * 1024 * 1024)


def next_slot(dest, slot, per_dest):
    slot = slot + 1
    wrap = slot == per_dest
    return jnp.where(wrap, dest + 1, dest), jnp.where(wrap, 0, slot)


def trial_kernel(size_ref, wave_ref, pot_ref, out_ref, field):
    sx, sy, sz = size_ref[0], size_ref[1], size_ref[2]
    per_dest = (sx * sy * sz) // (PEERS * 128)
    groups = sy // 16
    lane = lax.broadcasted_iota(jnp.int32, (8, 128), 1)
    z = lane % BOX
    low = lane < BOX
    live = (z < sz).astype(f32)
    has_next = (z < BOX - 1).astype(f32)
    has_last = (z > 0).astype(f32)
    zero = jnp.zeros((8, 128), f32)

    def fill(x, carry):
        base = 128 + (x + 1) * STRIDE
        field[:, pl.ds(aligned(base - 128), 128)] = zero
        field[:, pl.ds(aligned(base + sy * BOX), 128)] = zero

        def fill_group(g, c):
            for i in range(8):
                src = wave_ref[:, pl.ds(aligned(x * PLANE + g * 1024 + i * 128), 128)]
                field[:, pl.ds(aligned(base + g * 1024 + i * 128), 128)] = src.astype(f32) * live
            return c

        return lax.fori_loop(0, groups, fill_group, carry)

    lax.fori_loop(0, sx, fill, 0)

    def blank(i, carry):
        field[:, pl.ds(aligned(128 + i * 128), 128)] = zero
        field[:, pl.ds(aligned(128 + (sx + 1) * STRIDE + i * 128), 128)] = zero
        return carry

    lax.fori_loop(0, ROWS, blank, 0)

    def compute(x, g):
        base = 128 + (x + 1) * STRIDE + g * 1024
        parts = [field[:, pl.ds(aligned(base + (i - 1) * 128), 128)] for i in range(10)]
        turned = [pltpu.roll(p, BOX, 1) for p in parts]
        out = []
        for i in range(1, 9):
            c = parts[i]
            at = base + (i - 1) * 128
            beside = turned[i] + jnp.where(low, turned[i - 1], turned[i + 1])
            beside = beside + pltpu.roll(c, 127, 1) * has_next + pltpu.roll(c, 1, 1) * has_last
            beside = beside + field[:, pl.ds(aligned(at - STRIDE), 128)]
            beside = beside + field[:, pl.ds(aligned(at + STRIDE), 128)]
            pot = pot_ref[:, pl.ds(aligned(x * PLANE + g * 1024 + (i - 1) * 128), 128)]
            here = (1.0 - 3.0 * step_size) - step_size * pot
            out.append((c * here + (0.5 * step_size) * beside) * live)
        return out

    def emit(pieces, carry):
        dest, slot = carry
        for p in pieces:
            out_ref[dest, :, pl.ds(aligned(slot * 128), 128)] = p.astype(bf16)
            dest, slot = next_slot(dest, slot, per_dest)
        return dest, slot

    def planes(count, body):
        def outer(p, carry):
            return lax.fori_loop(0, groups, lambda g, c: body(p, g, c), carry)

        lax.fori_loop(0, count, outer, (jnp.int32(0), jnp.int32(0)))

    @pl.when(sz == 64)
    def _():
        planes(sx, lambda p, g, c: emit(compute(p, g), c))

    @pl.when(sz == 32)
    def _():
        def body(p, g, c):
            first, second = compute(2 * p, g), compute(2 * p + 1, g)
            return emit([a + pltpu.roll(b, 32, 1) for a, b in zip(first, second)], c)

        planes(sx // 2, body)

    @pl.when(sz == 48)
    def _():
        def body(p, g, c):
            last = compute(4 * p + 3, g)
            for j in range(3):
                part = ((z >= 16 * j) & (z < 16 * j + 16)).astype(f32)
                kept = compute(4 * p + j, g)
                c = emit([a + pltpu.roll(b * part, 48 - 16 * j, 1) for a, b in zip(kept, last)], c)
            return c

        planes(sx // 4, body)


def unpack_kernel(size_ref, in_ref, out_ref):
    sx, sy, sz = size_ref[0], size_ref[1], size_ref[2]
    per_dest = (sx * sy * sz) // (PEERS * 128)
    groups = sy // 16
    lane = lax.broadcasted_iota(jnp.int32, (8, 128), 1)
    z = lane % BOX
    live = (z < sz).astype(f32)

    @pl.when(per_dest < VOLUMES[-1])
    def _():
        def clear(i, carry):
            out_ref[:, pl.ds(aligned(i * 1024), 1024)] = jnp.zeros((8, 1024), bf16)
            return carry

        lax.fori_loop(0, CELLS // 1024, clear, 0)

    def take(carry):
        dest, slot = carry
        out = []
        for _ in range(8):
            out.append(in_ref[dest, :, pl.ds(aligned(slot * 128), 128)])
            dest, slot = next_slot(dest, slot, per_dest)
        return out, (dest, slot)

    def put(x, g, pieces):
        for i, p in enumerate(pieces):
            out_ref[:, pl.ds(aligned(x * PLANE + g * 1024 + i * 128), 128)] = p.astype(bf16)

    def planes(count, body):
        def outer(p, carry):
            return lax.fori_loop(0, groups, lambda g, c: body(p, g, c), carry)

        lax.fori_loop(0, count, outer, (jnp.int32(0), jnp.int32(0)))

    @pl.when(sz == 64)
    def _():
        def body(p, g, c):
            pieces, c = take(c)
            put(p, g, pieces)
            return c

        planes(sx, body)

    @pl.when(sz == 32)
    def _():
        def body(p, g, c):
            pieces, c = take(c)
            pieces = [a.astype(f32) for a in pieces]
            put(2 * p, g, [a * live for a in pieces])
            put(2 * p + 1, g, [pltpu.roll(a, 96, 1) * live for a in pieces])
            return c

        planes(sx // 2, body)

    @pl.when(sz == 48)
    def _():
        gap = (z >= 48).astype(f32)

        def body(p, g, c):
            last = [jnp.zeros((8, 128), f32)] * 8
            for j in range(3):
                pieces, c = take(c)
                pieces = [a.astype(f32) for a in pieces]
                put(4 * p + j, g, [a * live for a in pieces])
                last = [b + pltpu.roll(a * gap, 80 + 16 * j, 1) for a, b in zip(pieces, last)]
            put(4 * p + 3, g, last)
            return c

        planes(sx // 4, body)


def newton_kernel(gram_ref, out_ref):
    gram = gram_ref[...] * (1.0 / CELLS)
    frobenius = jnp.sqrt(jnp.sum(gram * gram, keepdims=True) + epsilon)
    row = lax.broadcasted_iota(jnp.int32, (NB, NB), 0)
    column = lax.broadcasted_iota(jnp.int32, (NB, NB), 1)
    three = jnp.where(row == column, 3.0, 0.0)
    dot = functools.partial(jnp.dot, precision=HIGHEST, preferred_element_type=f32)
    square = gram / frobenius
    step = 0.5 * (three - square)
    inverse = step
    square = dot(square, step)
    for sweep in range(1, NS_ITERS):
        step = 0.5 * (three - dot(inverse, square))
        if sweep < NS_ITERS - 1:
            square = dot(square, step)
        inverse = dot(step, inverse)
    out_ref[...] = (inverse / jnp.sqrt(frobenius)).T.astype(bf16)


def fresh_kernel(coeff_ref, rows_ref, occ_ref, out_ref, dens):
    step = pl.program_id(0)

    @pl.when(step < OWN)
    def _():
        fresh = jnp.dot(coeff_ref[...], rows_ref[...], preferred_element_type=f32)
        out_ref[...] = fresh.astype(bf16)
        dens[pl.ds(step, 1), :] = jnp.sum(occ_ref[...] * fresh * fresh, axis=0, keepdims=True) * (1.0 / NB)

    @pl.when(step == OWN)
    def _():
        block = dens[...].astype(bf16)
        for peer in range(PEERS):
            out_ref[peer * OWN : (peer + 1) * OWN, :] = block


def share_kernel(size_ref, offset_ref, where_ref, dens_ref, table_ref, out_ref, box):
    sx, sy, sz = size_ref[0], size_ref[1], size_ref[2]
    frag, band = where_ref[0], where_ref[1]
    groups = sy // 16
    lane = lax.broadcasted_iota(jnp.int32, (8, 128), 1)
    z = lane % BOX
    live = (z < sz).astype(f32)
    box[...] = jnp.zeros((BOX, 32, 128), f32)

    def tile(at):
        return dens_ref[pl.ds(pl.multiple_of(at * 8, 8), 8), :]

    def put(x, g, value):
        box[x, pl.ds(pl.multiple_of(g * 8, 8), 8), :] = value

    def planes(count, body):
        def outer(p, carry):
            return lax.fori_loop(0, groups, lambda g, c: body(p, g, c), carry)

        lax.fori_loop(0, count, outer, 0)

    @pl.when(sz == 64)
    def _():
        def body(p, g, c):
            put(p, g, tile(p * groups + g))
            return c

        planes(sx, body)

    @pl.when(sz == 32)
    def _():
        def body(p, g, c):
            value = tile(p * groups + g)
            put(2 * p, g, value * live)
            put(2 * p + 1, g, pltpu.roll(value, 96, 1) * live)
            return c

        planes(sx // 2, body)

    @pl.when(sz == 48)
    def _():
        gap = (z >= 48).astype(f32)

        def body(p, g, c):
            last = jnp.zeros((8, 128), f32)
            for j in range(3):
                value = tile((p * groups + g) * 3 + j)
                put(4 * p + j, g, value * live)
                last = last + pltpu.roll(value * gap, 80 + 16 * j, 1)
            put(4 * p + 3, g, last)
            return c

        planes(sx // 4, body)

    ox, oy = offset_ref[frag, 0], offset_ref[frag, 1]

    def plane(x):
        inside = ((x >= 0) & (x < sx)).astype(f32)
        return (box[jnp.clip(x, 0, BOX - 1)] * inside).astype(bf16)

    for i in range(4):
        value = plane(4 * band + i - ox)
        for other in range(8):
            out_ref[other, i * 32 : (i + 1) * 32, :] = value
    for other in range(8):
        for j in range(2):
            value = plane(offset_ref[other, 0] + 2 * band + j - ox)
            out_ref[other, (4 + j) * 32 : (5 + j) * 32, :] = value

    wide = lax.broadcasted_iota(jnp.int32, (32, 128), 1)
    even = table_ref[pl.ds(oy, 32, stride=2), :]
    odd = table_ref[pl.ds(oy + 1, 32, stride=2), :]
    weights = []
    for k in range(4):
        pick = wide == 4 * band + k
        first = jnp.sum(jnp.where(pick, even, 0.0), axis=1, keepdims=True)
        second = jnp.sum(jnp.where(pick, odd, 0.0), axis=1, keepdims=True)
        weights.append(jnp.where(wide < BOX, first, second))
    low = lane < BOX
    for pair in range(2):
        for part in range(4):
            rows = []
            for half in range(2):
                start = part * 16 + half * 8
                cube = box[start : start + 8]
                sums = []
                for k in (2 * pair, 2 * pair + 1):
                    s = jnp.sum(cube * weights[k][None], axis=1)
                    sums.append(s + pltpu.roll(s, BOX, 1))
                rows.append(jnp.where(low, sums[0], sums[1]))
            value = jnp.concatenate(rows, axis=0).astype(bf16)
            at = 192 + pair * BOX + part * 16
            for other in range(8):
                out_ref[other, at : at + 16, :] = value


def solve_kernel(offset_ref, sign_ref, where_ref, in_ref, table_ref, column_ref, row_ref, patched_ref, out_ref, placed, target, spread, along, cols, turned):
    frag, band = where_ref[0], where_ref[1]
    lane = lax.broadcasted_iota(jnp.int32, (32, 128), 1)
    low = lane < BOX
    wide = lax.broadcasted_iota(jnp.int32, (BOX, G), 1)
    line = lax.broadcasted_iota(jnp.int32, (BOX, G), 0)
    dot = functools.partial(lax.dot_general, preferred_element_type=f32)
    plain = (((1,), (0,)), ((), ()))
    across = (((0,), (0,)), ((), ()))
    half = (lax.broadcasted_iota(jnp.int32, (G, G), 1) < BOX).astype(f32)
    for f in range(8):
        ox, oy, oz = offset_ref[f, 0], offset_ref[f, 1], offset_ref[f, 2]
        sign = sign_ref[f].astype(f32)
        for i in range(6):
            value = in_ref[f, i * 32 : (i + 1) * 32, :].astype(f32)
            first = pltpu.roll(jnp.where(low, value, 0.0), oz, 1)
            second = pltpu.roll(jnp.where(low, 0.0, value), (oz + BOX) % G, 1)
            placed[f * BOX : f * BOX + 32, i * G : (i + 1) * G] = first.astype(bf16)
            placed[f * BOX + 32 : (f + 1) * BOX, i * G : (i + 1) * G] = second.astype(bf16)
        lands = oy + 2 * (line % 32) + line // 32
        target[f * BOX : (f + 1) * BOX, :] = jnp.where(wide == lands, sign, 0.0).astype(bf16)
        part = table_ref[pl.ds(oz, BOX), :]
        part = jnp.concatenate([part, part], axis=0)
        value = in_ref[f, 192:320, :].astype(f32)
        both = jnp.concatenate([value * half, value * (1.0 - half)], axis=0)
        both = dot(both, part, plain, precision=HIGHEST)
        for parity in range(2):
            for pair in range(2):
                k = 2 * pair + parity
                at = parity * G + pair * BOX
                spread[f * BOX : (f + 1) * BOX, k * G : (k + 1) * G] = both[at : at + BOX, :]
        along[f * BOX : (f + 1) * BOX, :] = table_ref[pl.ds(ox, BOX), :] * sign
    patched_ref[...] = dot(target[...], placed[...], across)
    spectrum = dot(along[...], spread[...], across, precision=HIGHEST)
    table = table_ref[0:G, :]
    ex = column_ref[...]
    ez = row_ref[...]
    spot = lax.broadcasted_iota(jnp.int32, (1, G), 1)
    scaled = []
    for k in range(4):
        ey = jnp.sum(jnp.where(spot == 4 * band + k, ez, 0.0), axis=1, keepdims=True)
        scaled.append(spectrum[:, k * G : (k + 1) * G] * (screening / (ex + ey + ez + screening)))
    solved = dot(table, jnp.concatenate(scaled, axis=1), plain, precision=HIGHEST)
    for k in range(4):
        cols[k, 0:G, :] = dot(solved[:, k * G : (k + 1) * G], table, plain, precision=HIGHEST)
        cols[k, G : G + BOX, :] = jnp.zeros((BOX, G), f32)
    ox = offset_ref[frag, 0]
    for k in range(4):
        for i in range(4):
            turned[i, pl.ds(k, 32, stride=4), :] = cols[k, pl.ds(i, 32, stride=4), :]
        for j in range(2):
            turned[4 + j, pl.ds(k, 32, stride=4), :] = cols[k, pl.ds(ox + j, 32, stride=2), :]
    for i in range(6):
        out_ref[:, i * G : (i + 1) * G] = turned[i].astype(bf16)


def total_kernel(size_ref, offset_ref, where_ref, in_ref, local_ref, table_ref, slab_ref, window_ref, rows):
    sx, sy, sz = size_ref[0], size_ref[1], size_ref[2]
    frag, band = where_ref[0], where_ref[1]
    oy, oz = offset_ref[frag, 1], offset_ref[frag, 2]
    table = table_ref[0:G, :]
    hartree = jnp.dot(table, in_ref[...].astype(f32), precision=HIGHEST, preferred_element_type=f32)
    total = hartree - local_ref[...]
    for i in range(4):
        slab_ref[i] = total[:, i * G : (i + 1) * G]
    lane = lax.broadcasted_iota(jnp.int32, (32, 128), 1)
    line = lax.broadcasted_iota(jnp.int32, (32, 128), 0)
    live = ((lane % BOX < sz) & (2 * line + lane // BOX < sy)).astype(f32)
    low = lane < BOX
    for j in range(2):
        rows[0:G, :] = total[:, (4 + j) * G : (5 + j) * G]
        rows[G : G + BOX, :] = jnp.zeros((BOX, G), f32)
        even = pltpu.roll(rows[pl.ds(oy, 32, stride=2), :], (G - oz) % G, 1)
        odd = pltpu.roll(rows[pl.ds(oy + 1, 32, stride=2), :], (G + BOX - oz) % G, 1)
        inside = (2 * band + j < sx).astype(f32)
        value = (jnp.where(low, even, odd) * live * inside).astype(bf16)
        for peer in range(PEERS):
            window_ref[peer, j * 32 : (j + 1) * 32, :] = value


def swap(block, axis="band"):
    return lax.all_to_all(block, axis, split_axis=0, concat_axis=0, tiled=True)


def swap_trial(volume, trial):
    lanes = volume * 128
    if lanes == FULL:
        return swap(trial)
    return jnp.pad(swap(trial[:, :, :lanes]), ((0, 0), (0, 0), (0, FULL - lanes)))


def swap_fresh(volume, block):
    lanes = volume * 128
    width = -(-volume // OWN) * 128
    if lanes == FULL:
        back = swap(block)
    else:
        dens = block[0, :, FULL:].reshape(FULL)[:lanes]
        dens = jnp.pad(dens, (0, OWN * width - lanes)).reshape(1, OWN, width)
        dens = jnp.broadcast_to(dens, (PEERS, OWN, width))
        back = swap(jnp.concatenate([block[:, :, :lanes], dens], axis=2))
    dens = back[:, :, lanes:].reshape(PEERS, OWN * width)[:, :lanes].reshape(PEERS * volume, 128)
    dens = jnp.pad(dens.astype(f32), ((0, CELLS // 128 - PEERS * volume), (0, 0)))
    back = jnp.pad(back, ((0, 0), (0, 0), (0, FULL + EXTRA - lanes - width)))
    return back, dens


def body(wave_coeffs, old_potential, occupations, box_sizes, box_offsets, patch_signs):
    fragment = lax.axis_index("frag")
    band_index = lax.axis_index("band")
    where = jnp.stack([fragment, band_index]).astype(jnp.int32)
    size = lax.dynamic_index_in_dim(box_sizes, fragment, 0, keepdims=False)
    volume = size[0] * size[1] * size[2] // (PEERS * 128)
    kind = jnp.sum((jnp.asarray(VOLUMES, jnp.int32) < volume).astype(jnp.int32))
    padded, eigen = sine_table()
    table = jnp.asarray(padded)
    eigen_row, eigen_column = jnp.asarray(eigen[None, :]), jnp.asarray(eigen[:, None])

    trial = pl.pallas_call(
        trial_kernel,
        out_shape=jax.ShapeDtypeStruct((PEERS, OWN, FULL), bf16),
        in_specs=[smem(), vmem(), vmem()],
        out_specs=vmem(),
        scratch_shapes=[pltpu.VMEM((8, 128 + (BOX + 2) * STRIDE), f32)],
        compiler_params=params(40),
        name="trial",
    )(size, wave_coeffs[0], old_potential)
    rows = lax.switch(kind, [functools.partial(swap_trial, v) for v in VOLUMES], trial)
    rows = rows.reshape(NB, FULL)
    partial_value = lax.dot_general(rows, rows, (((1,), (1,)), ((), ())), preferred_element_type=f32)
    share = swap(partial_value.reshape(PEERS, OWN, NB)).sum(axis=0)
    gram = swap(jnp.broadcast_to(share[None], (PEERS, OWN, NB))).reshape(NB, NB)
    coeff = pl.pallas_call(
        newton_kernel,
        out_shape=jax.ShapeDtypeStruct((NB, NB), bf16),
        in_specs=[vmem()],
        out_specs=vmem(),
        compiler_params=params(32),
        name="newton",
    )(gram)
    fresh = pl.pallas_call(
        fresh_kernel,
        out_shape=jax.ShapeDtypeStruct((NB, FULL + EXTRA), bf16),
        grid=(OWN + 1,),
        in_specs=[
            pl.BlockSpec((NB, NB), lambda j: (0, 0)),
            pl.BlockSpec((NB, EXTRA), lambda j: (0, jnp.minimum(j, OWN - 1))),
            pl.BlockSpec((NB, 1), lambda j: (0, 0)),
        ],
        out_specs=pl.BlockSpec((NB, EXTRA), lambda j: (0, j)),
        scratch_shapes=[pltpu.VMEM((OWN, EXTRA), f32)],
        compiler_params=params(32),
        name="fresh",
    )(coeff, rows, occupations.reshape(NB, 1))
    fresh = fresh.reshape(PEERS, OWN, FULL + EXTRA)
    back, dens = lax.switch(kind, [functools.partial(swap_fresh, v) for v in VOLUMES], fresh)
    shared = pl.pallas_call(
        share_kernel,
        out_shape=jax.ShapeDtypeStruct((8, 320, 128), bf16),
        in_specs=[smem(), smem(), smem(), vmem(), vmem()],
        out_specs=vmem(),
        scratch_shapes=[pltpu.VMEM((BOX, 32, 128), f32)],
        compiler_params=params(32),
        name="share",
    )(size, box_offsets, where, dens, table)
    parts = swap(shared, "frag")
    patched, columns = pl.pallas_call(
        solve_kernel,
        out_shape=(jax.ShapeDtypeStruct((G, 6 * G), f32), jax.ShapeDtypeStruct((G, 6 * G), bf16)),
        in_specs=[smem(), smem(), smem(), vmem(), vmem(), vmem(), vmem()],
        out_specs=(vmem(), vmem()),
        scratch_shapes=[
            pltpu.VMEM((8 * BOX, 6 * G), bf16),
            pltpu.VMEM((8 * BOX, G), bf16),
            pltpu.VMEM((8 * BOX, 4 * G), f32),
            pltpu.VMEM((8 * BOX, G), f32),
            pltpu.VMEM((4, G + BOX, G), f32),
            pltpu.VMEM((6, G, G), f32),
        ],
        compiler_params=params(32),
        name="solve",
    )(box_offsets, patch_signs, where, parts, table, eigen_column, eigen_row)
    columns = swap(columns.reshape(PEERS, 4, 6 * G)).reshape(G, 6 * G)
    local = local_factor * jnp.cbrt(jnp.maximum(patched, 0.0))
    total_potential, window = pl.pallas_call(
        total_kernel,
        out_shape=(jax.ShapeDtypeStruct((4, G, G), f32), jax.ShapeDtypeStruct((PEERS, 64, 128), bf16)),
        in_specs=[smem(), smem(), smem(), vmem(), vmem(), vmem()],
        out_specs=(vmem(), vmem()),
        scratch_shapes=[pltpu.VMEM((G + BOX, G), f32)],
        compiler_params=params(32),
        name="total",
    )(size, box_offsets, where, columns, local, table)
    window = swap(window)
    waves_out = pl.pallas_call(
        unpack_kernel,
        out_shape=jax.ShapeDtypeStruct((OWN, CELLS), bf16),
        in_specs=[smem(), vmem()],
        out_specs=vmem(),
        compiler_params=params(32),
        name="unpack",
    )(size, back)
    box_potential = window.astype(f32).reshape(1, CELLS)
    return (waves_out[None], box_potential, total_potential)


def solution(mesh):
    placed = (P("frag", "band", None), P("frag", None), P("frag", None), P(), P(), P())
    return jax.shard_map(
        body,
        mesh=mesh,
        in_specs=placed,
        out_specs=(P("frag", "band", None), P("frag", None), P("band", None, None)),
        check_vma=False,
    )
```

```python
import functools

import jax
import jax.numpy as jnp
import numpy as np
from jax import lax
from jax.experimental import pallas as pl
from jax.experimental.pallas import tpu as pltpu
from jax.sharding import PartitionSpec as P

NB = 256
BOX = 64
G = 128
NS_ITERS = 8
CELLS = BOX**3
PLANE = BOX * BOX
PEERS = 32
OWN = NB // PEERS
FULL = CELLS // PEERS
EXTRA = FULL // OWN
SIZES, OFFSETS, SIGNS, PLACE = 0, 24, 48, 56
VOLUMES = (8, 12, 16, 18, 24, 27, 32, 36, 48, 64)

step_size = 0.1
screening = 0.5
local_factor = 0.75
epsilon = 1e-06
HIGHEST = lax.Precision.HIGHEST
f32 = jnp.float32
bf16 = jnp.bfloat16


def sine_table():
    index = np.arange(G, dtype=np.float64) + 1.0
    table = np.sqrt(2.0 / (G + 1)) * np.sin(np.pi * index[:, None] * index[None, :] / (G + 1))
    eigen = 2.0 - 2.0 * np.cos(np.pi * index / (G + 1))
    padded = np.zeros((G + BOX, G), np.float32)
    padded[:G] = table
    return padded, eigen.astype(np.float32)


def aligned(offset):
    return pl.multiple_of(offset, 128)


def vmem():
    return pl.BlockSpec(memory_space=pltpu.VMEM)


def smem():
    return pl.BlockSpec(memory_space=pltpu.SMEM)


def box_size(meta):
    at = SIZES + 3 * meta[PLACE]
    return meta[at], meta[at + 1], meta[at + 2]


def box_offset(meta, f):
    at = OFFSETS + 3 * f
    return meta[at], meta[at + 1], meta[at + 2]


def params(mib):
    return pltpu.CompilerParams(vmem_limit_bytes=mib * 1024 * 1024)


def runs(total, run, per_dest, carry):
    dest, slot = carry
    places = []
    for _ in range(total // run):
        places.append((dest, slot))
        slot = slot + run
        wrap = slot == per_dest
        dest, slot = jnp.where(wrap, dest + 1, dest), jnp.where(wrap, 0, slot)
    return places, (dest, slot)


def each_part(size, per_dest, deep, body):
    sx, sy, sz = size
    run = {64: 4, 32: 2, 48: 1}[deep]

    @pl.when((sz == deep) & (per_dest < VOLUMES[-1]))
    def _():
        def quad(q, carry):
            def part(g, place):
                places, place = runs(deep // 2, run, per_dest, place)

                def at(plane, i):
                    dest, slot = places[(plane * 8 + i) // run]
                    return dest, aligned((slot + i % run) * 128)

                body(4 * q, g, at)
                return place

            return lax.fori_loop(0, sy // 16, part, carry)

        lax.fori_loop(0, sx // 4, quad, (jnp.int32(0), jnp.int32(0)))


def full_place(q, plane, i):
    flat = i // 8 * 32 + plane * 8 + i % 8
    return 2 * q + flat // 64, flat % 64 * 128


def trial_kernel(meta, wave_ref, pot_ref, out_ref, kind_ref, held):
    size = box_size(meta)
    sx, sy, sz = size
    per_dest = (sx * sy * sz) // (PEERS * 128)
    kind = jnp.int32(0)
    for volume in VOLUMES:
        kind = kind + (volume < per_dest).astype(jnp.int32)
    kind_ref[0] = kind
    lane = lax.broadcasted_iota(jnp.int32, (8, 128), 1)
    z = lane % BOX
    low = lane < BOX
    has_last = (z > 0).astype(f32)
    zero = jnp.zeros((8, 128), f32)

    def load(x, i):
        return wave_ref[:, pl.ds(aligned(x * PLANE + i * 128), 128)].astype(f32)

    def edges(x):
        before = jnp.where(x > 0, 1.0, 0.0)
        after = jnp.where(x + 4 < sx, 1.0, 0.0)
        return before, after, jnp.maximum(x - 1, 0), jnp.minimum(x + 4, BOX - 1)

    def stencil(c, turned, last_turned, next_turned, around, has_next, x, i):
        beside = turned + jnp.where(low, last_turned, next_turned)
        beside = beside + (pltpu.roll(c, 127, 1) * has_next + pltpu.roll(c, 1, 1) * has_last)
        beside = beside + around
        pot = pot_ref[:, pl.ds(aligned(x * PLANE + i * 128), 128)]
        return c * ((1.0 - 3.0 * step_size) - step_size * pot) + (0.5 * step_size) * beside

    @pl.when(per_dest == VOLUMES[-1])
    def _():
        has_next = (z < BOX - 1).astype(f32)

        def quad(q, carry):
            x = 4 * q
            before, after, xb, xa = edges(x)
            last_turned, here = [zero] * 4, [load(x + p, 0) for p in range(4)]
            turned = [pltpu.roll(c, BOX, 1) for c in here]
            for i in range(32):
                ahead = [load(x + p, i + 1) for p in range(4)] if i < 31 else [zero] * 4
                ahead_turned = [pltpu.roll(c, BOX, 1) for c in ahead] if i < 31 else [zero] * 4
                line = [load(xb, i) * before] + here + [load(xa, i) * after]
                for p in range(4):
                    around = line[p] + line[p + 2]
                    value = stencil(here[p], turned[p], last_turned[p], ahead_turned[p], around, has_next, x + p, i)
                    dest, slot = full_place(q, p, i)
                    out_ref[dest, :, slot : slot + 128] = value.astype(bf16)
                here, last_turned, turned = ahead, turned, ahead_turned
            return carry

        lax.fori_loop(0, BOX // 4, quad, 0)

    def some(deep):
        live = (z < deep).astype(f32)
        has_next = (z < deep - 1).astype(f32)

        def part(x, g, at):
            before, after, xb, xa = edges(x)
            top = jnp.where(g > 0, 1.0, 0.0)
            bottom = jnp.where(16 * g + 16 < sy, 1.0, 0.0)
            first, last = jnp.maximum(8 * g - 1, 0), jnp.minimum(8 * g + 8, 31)
            lines = []
            for p in range(4):
                inner = [load(x + p, 8 * g + i) for i in range(8)]
                lines.append([load(x + p, first) * top] + inner + [load(x + p, last) * bottom])
            turned = [[pltpu.roll(c, BOX, 1) for c in line] for line in lines]
            for i in range(8):
                line = [load(xb, 8 * g + i) * before] + [lines[p][i + 1] for p in range(4)] + [load(xa, 8 * g + i) * after]
                for p in range(4):
                    t = turned[p]
                    around = line[p] + line[p + 2]
                    value = stencil(line[p + 1], t[i + 1], t[i], t[i + 2], around, has_next, x + p, 8 * g + i)
                    if deep == BOX:
                        dest, slot = at(p, i)
                        out_ref[dest, :, pl.ds(slot, 128)] = value.astype(bf16)
                    else:
                        held[:, p * 1024 + i * 128 : p * 1024 + (i + 1) * 128] = value * live
            if deep == BOX:
                return

            def kept(p, i):
                return held[:, p * 1024 + i * 128 : p * 1024 + (i + 1) * 128]

            for i in range(8):
                for p in range(deep // 16):
                    if deep == 32:
                        value = kept(2 * p, i) + pltpu.roll(kept(2 * p + 1, i), 32, 1)
                    else:
                        piece = (z >= 16 * p) & (z < 16 * p + 16)
                        value = kept(p, i) + pltpu.roll(jnp.where(piece, kept(3, i), 0.0), 48 - 16 * p, 1)
                    dest, slot = at(p, i)
                    out_ref[dest, :, pl.ds(slot, 128)] = value.astype(bf16)

        each_part(size, per_dest, deep, part)

    for deep in (32, 48, 64):
        some(deep)


def unpack_kernel(meta, in_ref, out_ref):
    size = box_size(meta)
    sx, sy, sz = size
    per_dest = (sx * sy * sz) // (PEERS * 128)
    lane = lax.broadcasted_iota(jnp.int32, (8, 128), 1)
    z = lane % BOX

    def put(x, i, value):
        out_ref[:, pl.ds(aligned(x * PLANE + i * 128), 128)] = value.astype(bf16)

    @pl.when(per_dest == VOLUMES[-1])
    def _():
        def quad(q, carry):
            for i in range(32):
                for p in range(4):
                    dest, slot = full_place(q, p, i)
                    put(4 * q + p, i, in_ref[dest, :, slot : slot + 128])
            return carry

        lax.fori_loop(0, BOX // 4, quad, 0)

    @pl.when(per_dest < VOLUMES[-1])
    def _():
        def clear(i, carry):
            out_ref[:, pl.ds(aligned(i * PLANE), PLANE)] = jnp.zeros((8, PLANE), bf16)
            return carry

        lax.fori_loop(0, BOX, clear, 0)

    def some(deep):
        live = (z < deep).astype(f32)
        gap = (z >= deep).astype(f32)

        def part(x, g, at):
            for i in range(8):
                row = 8 * g + i
                values = []
                for p in range(deep // 16):
                    dest, slot = at(p, i)
                    values.append(in_ref[dest, :, pl.ds(slot, 128)])
                if deep == 64:
                    for p in range(4):
                        put(x + p, row, values[p])
                    continue
                values = [value.astype(f32) for value in values]
                if deep == 32:
                    for p in range(2):
                        put(x + 2 * p, row, values[p] * live)
                        put(x + 2 * p + 1, row, pltpu.roll(values[p], 96, 1) * live)
                else:
                    for p in range(3):
                        put(x + p, row, values[p] * live)
                    rest = [pltpu.roll(values[p] * gap, 80 + 16 * p, 1) for p in range(3)]
                    put(x + 3, row, rest[0] + rest[1] + rest[2])

        each_part(size, per_dest, deep, part)

    for deep in (32, 48, 64):
        some(deep)


def gram_kernel(rows_ref, out_ref, blocks, arrived):
    copies = []
    for i in range(OWN):
        part = rows_ref.at[:, i * EXTRA : (i + 1) * EXTRA]
        copies.append(pltpu.make_async_copy(part, blocks.at[i], arrived.at[i]))
        copies[-1].start()
    total = jnp.zeros((NB, NB), f32)
    for i in range(OWN):
        copies[i].wait()
        block = blocks[i]
        total = total + lax.dot_general(block, block, (((1,), (1,)), ((), ())), preferred_element_type=f32)
    out_ref[...] = total


def halves(value):
    head = value.astype(bf16)
    return head, (value - head.astype(f32)).astype(bf16)


def product(left, right):
    dot = functools.partial(jnp.dot, preferred_element_type=f32)
    return dot(left[0], right[0]) + (dot(left[0], right[1]) + dot(left[1], right[0]))


def newton_kernel(gram_ref, out_ref):
    gram = gram_ref[...] * (1.0 / CELLS)
    frobenius = jnp.sqrt(jnp.sum(gram * gram, keepdims=True) + epsilon)
    row = lax.broadcasted_iota(jnp.int32, (NB, NB), 0)
    column = lax.broadcasted_iota(jnp.int32, (NB, NB), 1)
    three = jnp.where(row == column, 1.5, 0.0)
    square = gram / frobenius
    step = halves(three - 0.5 * square)
    inverse = step
    square = halves(product(halves(square), step))
    for sweep in range(1, NS_ITERS):
        step = halves(three - 0.5 * product(inverse, square))
        if sweep < NS_ITERS - 1:
            square = halves(product(square, step))
        inverse = product(step, inverse)
        if sweep < NS_ITERS - 1:
            inverse = halves(inverse)
    out_ref[...] = (inverse / jnp.sqrt(frobenius)).T.astype(bf16)


def fresh_kernel(coeff_ref, rows_ref, occ_ref, out_ref, dens, weight):
    step = pl.program_id(0)

    @pl.when(step == 0)
    def _():
        weight[...] = jnp.broadcast_to(occ_ref[...] * (1.0 / NB), (128, NB)).T

    @pl.when(step < OWN)
    def _():
        fresh = jnp.dot(coeff_ref[...], rows_ref[...], preferred_element_type=f32)
        out_ref[...] = fresh.astype(bf16)
        sums = jnp.sum(weight[:, 0:1] * fresh * fresh, axis=0, keepdims=True)
        for i in range(8):
            dens[i : i + 1, pl.ds(aligned(step * 128), 128)] = sums[:, i * 128 : (i + 1) * 128]

    @pl.when(step == OWN)
    def _():
        block = dens[...].astype(bf16)
        for peer in range(PEERS):
            out_ref[peer * OWN : (peer + 1) * OWN, :] = block


def share_kernel(meta, dens_ref, table_ref, out_ref, box):
    sx, sy, sz = box_size(meta)
    frag, band = meta[PLACE], meta[PLACE + 1]
    groups = sy // 16
    lane = lax.broadcasted_iota(jnp.int32, (8, 128), 1)
    z = lane % BOX
    live = (z < sz).astype(f32)
    box[...] = jnp.zeros((BOX, 32, 128), f32)

    def tile(at):
        return dens_ref[at // 8, :, pl.ds(aligned(at % 8 * 128), 128)].astype(f32)

    def put(x, g, value):
        box[x, pl.ds(pl.multiple_of(g * 8, 8), 8), :] = value

    def parts(deep, body):
        @pl.when(sz == deep)
        def _():
            def outer(q, carry):
                def inner(g, c):
                    body(4 * q, g, [tile((q * groups + g) * (deep // 16) + p) for p in range(deep // 16)])
                    return c

                return lax.fori_loop(0, groups, inner, carry)

            lax.fori_loop(0, sx // 4, outer, 0)

    def whole(x, g, values):
        for p in range(4):
            put(x + p, g, values[p])

    def half(x, g, values):
        for p in range(2):
            put(x + 2 * p, g, values[p] * live)
            put(x + 2 * p + 1, g, pltpu.roll(values[p], 96, 1) * live)

    def most(x, g, values):
        gap = (z >= 48).astype(f32)
        for p in range(3):
            put(x + p, g, values[p] * live)
        rest = [pltpu.roll(values[p] * gap, 80 + 16 * p, 1) for p in range(3)]
        put(x + 3, g, rest[0] + rest[1] + rest[2])

    parts(64, whole)
    parts(32, half)
    parts(48, most)

    ox, oy, _ = box_offset(meta, frag)

    def plane(x):
        inside = ((x >= 0) & (x < sx)).astype(f32)
        return (box[jnp.clip(x, 0, BOX - 1)] * inside).astype(bf16)

    for i in range(4):
        value = plane(4 * band + i - ox)
        for other in range(8):
            out_ref[other, i * 32 : (i + 1) * 32, :] = value
    for other in range(8):
        for j in range(2):
            value = plane(box_offset(meta, other)[0] + 2 * band + j - ox)
            out_ref[other, (4 + j) * 32 : (5 + j) * 32, :] = value

    wide = lax.broadcasted_iota(jnp.int32, (32, 128), 1)
    even = table_ref[pl.ds(oy, 32, stride=2), :]
    odd = table_ref[pl.ds(oy + 1, 32, stride=2), :]
    weights = []
    for k in range(4):
        pick = wide == 4 * band + k
        first = jnp.sum(jnp.where(pick, even, 0.0), axis=1, keepdims=True)
        second = jnp.sum(jnp.where(pick, odd, 0.0), axis=1, keepdims=True)
        weights.append(jnp.where(wide < BOX, first, second))
    low = lane < BOX
    for pair in range(2):
        for part in range(4):
            rows = []
            for half in range(2):
                start = part * 16 + half * 8
                cube = box[start : start + 8]
                sums = []
                for k in (2 * pair, 2 * pair + 1):
                    s = jnp.sum(cube * weights[k][None], axis=1)
                    sums.append(s + pltpu.roll(s, BOX, 1))
                rows.append(jnp.where(low, sums[0], sums[1]))
            value = jnp.concatenate(rows, axis=0).astype(bf16)
            at = 192 + pair * BOX + part * 16
            for other in range(8):
                out_ref[other, at : at + 16, :] = value


def solve_kernel(meta, in_ref, table_ref, column_ref, row_ref, patched_ref, out_ref, placed, target, spread, along, cols, turned):
    frag, band = meta[PLACE], meta[PLACE + 1]
    lane = lax.broadcasted_iota(jnp.int32, (32, 128), 1)
    low = lane < BOX
    wide = lax.broadcasted_iota(jnp.int32, (BOX, G), 1)
    line = lax.broadcasted_iota(jnp.int32, (BOX, G), 0)
    dot = functools.partial(lax.dot_general, preferred_element_type=f32)
    plain = (((1,), (0,)), ((), ()))
    across = (((0,), (0,)), ((), ()))
    half = (lax.broadcasted_iota(jnp.int32, (G, G), 1) < BOX).astype(f32)
    for f in range(8):
        ox, oy, oz = box_offset(meta, f)
        sign = meta[SIGNS + f].astype(f32)
        for i in range(6):
            value = in_ref[f, i * 32 : (i + 1) * 32, :].astype(f32)
            first = pltpu.roll(jnp.where(low, value, 0.0), oz, 1)
            second = pltpu.roll(jnp.where(low, 0.0, value), (oz + BOX) % G, 1)
            placed[f * BOX : f * BOX + 32, i * G : (i + 1) * G] = first.astype(bf16)
            placed[f * BOX + 32 : (f + 1) * BOX, i * G : (i + 1) * G] = second.astype(bf16)
        lands = oy + 2 * (line % 32) + line // 32
        target[f * BOX : (f + 1) * BOX, :] = jnp.where(wide == lands, sign, 0.0).astype(bf16)
        part = table_ref[pl.ds(oz, BOX), :]
        part = jnp.concatenate([part, part], axis=0)
        value = in_ref[f, 192:320, :].astype(f32)
        both = jnp.concatenate([value * half, value * (1.0 - half)], axis=0)
        both = dot(both, part, plain, precision=HIGHEST)
        for parity in range(2):
            for pair in range(2):
                k = 2 * pair + parity
                at = parity * G + pair * BOX
                spread[f * BOX : (f + 1) * BOX, k * G : (k + 1) * G] = both[at : at + BOX, :]
        along[f * BOX : (f + 1) * BOX, :] = table_ref[pl.ds(ox, BOX), :] * sign
    patched_ref[...] = dot(target[...], placed[...], across)
    spectrum = dot(along[...], spread[...], across, precision=HIGHEST)
    table = table_ref[0:G, :]
    ex = column_ref[...]
    ez = row_ref[...]
    spot = lax.broadcasted_iota(jnp.int32, (1, G), 1)
    scaled = []
    for k in range(4):
        ey = jnp.sum(jnp.where(spot == 4 * band + k, ez, 0.0), axis=1, keepdims=True)
        scaled.append(spectrum[:, k * G : (k + 1) * G] * (screening / (ex + ey + ez + screening)))
    solved = dot(table, jnp.concatenate(scaled, axis=1), plain, precision=HIGHEST)
    for k in range(4):
        cols[k, 0:G, :] = dot(solved[:, k * G : (k + 1) * G], table, plain, precision=HIGHEST)
        cols[k, G : G + BOX, :] = jnp.zeros((BOX, G), f32)
    ox = box_offset(meta, frag)[0]
    for k in range(4):
        for i in range(6):
            part = cols[k, pl.ds(i, 32, stride=4), :] if i < 4 else cols[k, pl.ds(ox + i - 4, 32, stride=2), :]
            turned[i % 3, pl.ds(2 * k + i // 3, 32, stride=8), :] = part
    for i in range(3):
        out_ref[:, i * G : (i + 1) * G] = turned[i].astype(bf16)


def total_kernel(meta, in_ref, local_ref, table_ref, slab_ref, window_ref, columns, rows):
    sx, sy, sz = box_size(meta)
    frag, band = meta[PLACE], meta[PLACE + 1]
    _, oy, oz = box_offset(meta, frag)
    table = table_ref[0:G, :]
    for i in range(3):
        columns[i] = in_ref[:, i * G : (i + 1) * G].astype(f32)

    def total(i):
        part = columns[i % 3, pl.ds(i // 3, G, stride=2), :]
        hartree = jnp.dot(table, part, precision=HIGHEST, preferred_element_type=f32)
        return hartree - local_ref[:, i * G : (i + 1) * G]

    for i in range(4):
        slab_ref[i] = total(i)
    lane = lax.broadcasted_iota(jnp.int32, (32, 128), 1)
    line = lax.broadcasted_iota(jnp.int32, (32, 128), 0)
    live = ((lane % BOX < sz) & (2 * line + lane // BOX < sy)).astype(f32)
    low = lane < BOX
    for j in range(2):
        rows[0:G, :] = total(4 + j)
        rows[G : G + BOX, :] = jnp.zeros((BOX, G), f32)
        even = pltpu.roll(rows[pl.ds(oy, 32, stride=2), :], (G - oz) % G, 1)
        odd = pltpu.roll(rows[pl.ds(oy + 1, 32, stride=2), :], (G + BOX - oz) % G, 1)
        inside = (2 * band + j < sx).astype(f32)
        value = (jnp.where(low, even, odd) * live * inside).astype(bf16)
        for peer in range(PEERS):
            window_ref[peer, j * 32 : (j + 1) * 32, :] = value


def swap(block, axis="band"):
    return lax.all_to_all(block, axis, split_axis=0, concat_axis=0, tiled=True)


def swap_trial(volume, trial):
    lanes = volume * 128
    if lanes == FULL:
        return swap(trial)
    return jnp.pad(swap(trial[:, :, :lanes]), ((0, 0), (0, 0), (0, FULL - lanes)))


def swap_fresh(volume, block):
    lanes = volume * 128
    if lanes == FULL:
        return swap(block)
    tiles = -(-volume // OWN)
    width = tiles * 128
    back = swap(jnp.concatenate([block[:, :, :lanes], block[:, :, FULL : FULL + width]], axis=2))
    dens = back[:, :, lanes:].reshape(PEERS, OWN, tiles, 128).transpose(0, 2, 1, 3).reshape(PEERS, OWN * width)
    dens = jnp.pad(dens[:, :lanes].reshape(PEERS * lanes), (0, CELLS - PEERS * lanes))
    dens = dens.reshape(PEERS, OWN, OWN, 128).transpose(0, 2, 1, 3).reshape(PEERS, OWN, EXTRA)
    return jnp.concatenate([jnp.pad(back[:, :, :lanes], ((0, 0), (0, 0), (0, FULL - lanes))), dens], axis=2)


def body(wave_coeffs, old_potential, occupations, box_sizes, box_offsets, patch_signs):
    fragment = lax.axis_index("frag")
    band_index = lax.axis_index("band")
    scalars = [box_sizes.reshape(24), box_offsets.reshape(24), patch_signs, jnp.stack([fragment, band_index])]
    meta = jnp.concatenate([part.astype(jnp.int32) for part in scalars])
    padded, eigen = sine_table()
    table = jnp.asarray(padded)
    eigen_row, eigen_column = jnp.asarray(eigen[None, :]), jnp.asarray(eigen[:, None])

    trial, kind = pl.pallas_call(
        trial_kernel,
        out_shape=(jax.ShapeDtypeStruct((PEERS, OWN, FULL), bf16), jax.ShapeDtypeStruct((1,), jnp.int32)),
        in_specs=[smem(), vmem(), vmem()],
        out_specs=(vmem(), smem()),
        scratch_shapes=[pltpu.VMEM((OWN, 4096), f32)],
        compiler_params=params(32),
        name="trial",
    )(meta, wave_coeffs[0], old_potential)
    kind = kind[0]
    rows = lax.switch(kind, [functools.partial(swap_trial, v) for v in VOLUMES], trial)
    rows = rows.reshape(NB, FULL)
    partial_value = pl.pallas_call(
        gram_kernel,
        out_shape=jax.ShapeDtypeStruct((NB, NB), f32),
        in_specs=[pl.BlockSpec(memory_space=pltpu.HBM)],
        out_specs=vmem(),
        scratch_shapes=[pltpu.VMEM((OWN, NB, EXTRA), bf16), pltpu.SemaphoreType.DMA((OWN,))],
        compiler_params=params(32),
        name="gram",
    )(rows)
    share = swap(partial_value.reshape(PEERS, OWN, NB)).sum(axis=0)
    gram = swap(jnp.broadcast_to(share[None], (PEERS, OWN, NB))).reshape(NB, NB)
    coeff = pl.pallas_call(
        newton_kernel,
        out_shape=jax.ShapeDtypeStruct((NB, NB), bf16),
        in_specs=[vmem()],
        out_specs=vmem(),
        compiler_params=params(32),
        name="newton",
    )(gram)
    fresh = pl.pallas_call(
        fresh_kernel,
        out_shape=jax.ShapeDtypeStruct((NB, FULL + EXTRA), bf16),
        grid=(OWN + 1,),
        in_specs=[
            pl.BlockSpec((NB, NB), lambda j: (0, 0)),
            pl.BlockSpec((NB, EXTRA), lambda j: (0, jnp.minimum(j, OWN - 1))),
            pl.BlockSpec((1, NB), lambda j: (0, 0)),
        ],
        out_specs=pl.BlockSpec((NB, EXTRA), lambda j: (0, j)),
        scratch_shapes=[pltpu.VMEM((OWN, EXTRA), f32), pltpu.VMEM((NB, 128), f32)],
        compiler_params=params(32),
        name="fresh",
    )(coeff, rows, occupations)
    fresh = fresh.reshape(PEERS, OWN, FULL + EXTRA)
    back = lax.switch(kind, [functools.partial(swap_fresh, v) for v in VOLUMES], fresh)
    shared = pl.pallas_call(
        share_kernel,
        out_shape=jax.ShapeDtypeStruct((8, 320, 128), bf16),
        grid=(1,),
        in_specs=[
            smem(),
            pl.BlockSpec((PEERS, OWN, EXTRA), lambda i: (0, 0, FULL // EXTRA)),
            pl.BlockSpec((G + BOX, G), lambda i: (0, 0)),
        ],
        out_specs=pl.BlockSpec((8, 320, 128), lambda i: (0, 0, 0)),
        scratch_shapes=[pltpu.VMEM((BOX, 32, 128), f32)],
        compiler_params=params(32),
        name="share",
    )(meta, back, table)
    parts = swap(shared, "frag")
    patched, columns = pl.pallas_call(
        solve_kernel,
        out_shape=(jax.ShapeDtypeStruct((G, 6 * G), f32), jax.ShapeDtypeStruct((2 * G, 3 * G), bf16)),
        in_specs=[smem(), vmem(), vmem(), vmem(), vmem()],
        out_specs=(vmem(), vmem()),
        scratch_shapes=[
            pltpu.VMEM((8 * BOX, 6 * G), bf16),
            pltpu.VMEM((8 * BOX, G), bf16),
            pltpu.VMEM((8 * BOX, 4 * G), f32),
            pltpu.VMEM((8 * BOX, G), f32),
            pltpu.VMEM((4, G + BOX, G), f32),
            pltpu.VMEM((3, 2 * G, G), f32),
        ],
        compiler_params=params(32),
        name="solve",
    )(meta, parts, table, eigen_column, eigen_row)
    columns = swap(columns.reshape(PEERS, 8, 3 * G)).reshape(2 * G, 3 * G)
    local = local_factor * jnp.cbrt(jnp.maximum(patched, 0.0))
    total_potential, window = pl.pallas_call(
        total_kernel,
        out_shape=(jax.ShapeDtypeStruct((4, G, G), f32), jax.ShapeDtypeStruct((PEERS, 64, 128), bf16)),
        in_specs=[smem(), vmem(), vmem(), vmem()],
        out_specs=(vmem(), vmem()),
        scratch_shapes=[pltpu.VMEM((3, 2 * G, G), f32), pltpu.VMEM((G + BOX, G), f32)],
        compiler_params=params(32),
        name="total",
    )(meta, columns, local, table)
    window = swap(window)
    waves_out = pl.pallas_call(
        unpack_kernel,
        out_shape=jax.ShapeDtypeStruct((OWN, CELLS), bf16),
        in_specs=[smem(), vmem()],
        out_specs=vmem(),
        compiler_params=params(32),
        name="unpack",
    )(meta, back)
    box_potential = window.astype(f32).reshape(1, CELLS)
    return (waves_out[None], box_potential, total_potential)


def solution(mesh):
    placed = (P("frag", "band", None), P("frag", None), P("frag", None), P(), P(), P())
    return jax.shard_map(
        body,
        mesh=mesh,
        in_specs=placed,
        out_specs=(P("frag", "band", None), P("frag", None), P("band", None, None)),
        check_vma=False,
    )
```

```python
import functools

import jax
import jax.numpy as jnp
import numpy as np
from jax import lax
from jax.experimental import pallas as pl
from jax.experimental.pallas import tpu as pltpu
from jax.sharding import PartitionSpec as P

NB = 256
BOX = 64
G = 128
NS_ITERS = 8
CELLS = BOX**3
PLANE = BOX * BOX
PEERS = 32
OWN = NB // PEERS
FULL = CELLS // PEERS
EXTRA = FULL // OWN
SIZES, OFFSETS, SIGNS, PLACE = 0, 3, 6, 7
VOLUMES = (8, 12, 16, 18, 24, 27, 32, 36, 48, 64)

step_size = 0.1
screening = 0.5
local_factor = 0.75
epsilon = 1e-06
f32 = jnp.float32
bf16 = jnp.bfloat16


def sine_table():
    index = np.arange(G, dtype=np.float64) + 1.0
    table = np.sqrt(2.0 / (G + 1)) * np.sin(np.pi * index[:, None] * index[None, :] / (G + 1))
    eigen = 2.0 - 2.0 * np.cos(np.pi * index / (G + 1))
    padded = np.zeros((G + BOX, G), np.float32)
    padded[:G] = table
    return padded, eigen.astype(np.float32)


def aligned(offset):
    return pl.multiple_of(offset, 128)


def vmem():
    return pl.BlockSpec(memory_space=pltpu.VMEM)


def smem():
    return pl.BlockSpec(memory_space=pltpu.SMEM)


def box_size(meta):
    f = meta[PLACE, 0]
    return meta[SIZES, f], meta[SIZES + 1, f], meta[SIZES + 2, f]


def box_offset(meta, f):
    return meta[OFFSETS, f], meta[OFFSETS + 1, f], meta[OFFSETS + 2, f]


def params(mib):
    return pltpu.CompilerParams(vmem_limit_bytes=mib * 1024 * 1024)


def runs(total, run, per_dest, carry):
    dest, slot = carry
    places = []
    for _ in range(total // run):
        places.append((dest, slot))
        slot = slot + run
        wrap = slot == per_dest
        dest, slot = jnp.where(wrap, dest + 1, dest), jnp.where(wrap, 0, slot)
    return places, (dest, slot)


def each_part(size, per_dest, deep, body, ready=None):
    sx, sy, sz = size
    run = {64: 4, 32: 2, 48: 1}[deep]

    @pl.when((sz == deep) & (per_dest < VOLUMES[-1]))
    def _():
        def quad(q, carry):
            if ready is not None:
                ready(q + 1)

            def part(g, place):
                places, place = runs(deep // 2, run, per_dest, place)

                def at(plane, i):
                    dest, slot = places[(plane * 8 + i) // run]
                    return dest, aligned((slot + i % run) * 128)

                body(4 * q, g, at)
                return place

            return lax.fori_loop(0, sy // 16, part, carry)

        lax.fori_loop(0, sx // 4, quad, (jnp.int32(0), jnp.int32(0)))


def full_place(q, plane, i):
    flat = i // 8 * 32 + plane * 8 + i % 8
    return 2 * q + flat // 64, flat % 64 * 128


def trial_kernel(meta, wave_in, pot_in, out_ref, kind_ref, held, wave_ref, pot_ref, arrived):
    size = box_size(meta)
    sx, sy, sz = size
    per_dest = (sx * sy * sz) // (PEERS * 128)
    kind = jnp.int32(0)
    for volume in VOLUMES:
        kind = kind + (volume < per_dest).astype(jnp.int32)
    kind_ref[0] = kind
    quads = sx // 4

    def fetch(q):
        lanes = pl.ds(aligned(q * 4 * PLANE), 4 * PLANE)
        wave = pltpu.make_async_copy(wave_in.at[:, lanes], wave_ref.at[:, lanes], arrived.at[0, q])
        return wave, pltpu.make_async_copy(pot_in.at[:, lanes], pot_ref.at[:, lanes], arrived.at[1, q])

    def begin(q, carry):
        for copy in fetch(q):
            copy.start()
        return carry

    def ready(q):
        @pl.when(q < quads)
        def _():
            for copy in fetch(q):
                copy.wait()

    lax.fori_loop(0, quads, begin, 0)
    ready(0)
    lane = lax.broadcasted_iota(jnp.int32, (8, 128), 1)
    z = lane % BOX
    low = lane < BOX
    has_last = (z > 0).astype(f32)
    zero = jnp.zeros((8, 128), f32)

    def load(x, i):
        return wave_ref[:, pl.ds(aligned(x * PLANE + i * 128), 128)].astype(f32)

    def edges(x):
        before = jnp.where(x > 0, 1.0, 0.0)
        after = jnp.where(x + 4 < sx, 1.0, 0.0)
        return before, after, jnp.maximum(x - 1, 0), jnp.minimum(x + 4, sx - 1)

    def stencil(c, turned, last_turned, next_turned, around, has_next, x, i):
        beside = turned + jnp.where(low, last_turned, next_turned)
        beside = beside + (pltpu.roll(c, 127, 1) * has_next + pltpu.roll(c, 1, 1) * has_last)
        beside = beside + around
        pot = pot_ref[:, pl.ds(aligned(x * PLANE + i * 128), 128)]
        return c * ((1.0 - 3.0 * step_size) - step_size * pot) + (0.5 * step_size) * beside

    @pl.when(per_dest == VOLUMES[-1])
    def _():
        has_next = (z < BOX - 1).astype(f32)

        def quad(q, carry):
            ready(q + 1)
            x = 4 * q
            before, after, xb, xa = edges(x)
            last_turned, here = [zero] * 4, [load(x + p, 0) for p in range(4)]
            turned = [pltpu.roll(c, BOX, 1) for c in here]
            for i in range(32):
                ahead = [load(x + p, i + 1) for p in range(4)] if i < 31 else [zero] * 4
                ahead_turned = [pltpu.roll(c, BOX, 1) for c in ahead] if i < 31 else [zero] * 4
                line = [load(xb, i) * before] + here + [load(xa, i) * after]
                for p in range(4):
                    around = line[p] + line[p + 2]
                    value = stencil(here[p], turned[p], last_turned[p], ahead_turned[p], around, has_next, x + p, i)
                    dest, slot = full_place(q, p, i)
                    out_ref[dest, :, slot : slot + 128] = value.astype(bf16)
                here, last_turned, turned = ahead, turned, ahead_turned
            return carry

        lax.fori_loop(0, BOX // 4, quad, 0)

    def some(deep):
        live = (z < deep).astype(f32)
        has_next = (z < deep - 1).astype(f32)

        def part(x, g, at):
            before, after, xb, xa = edges(x)
            top = jnp.where(g > 0, 1.0, 0.0)
            bottom = jnp.where(16 * g + 16 < sy, 1.0, 0.0)
            first, last = jnp.maximum(8 * g - 1, 0), jnp.minimum(8 * g + 8, 31)
            lines = []
            for p in range(4):
                inner = [load(x + p, 8 * g + i) for i in range(8)]
                lines.append([load(x + p, first) * top] + inner + [load(x + p, last) * bottom])
            turned = [[pltpu.roll(c, BOX, 1) for c in line] for line in lines]
            for i in range(8):
                line = [load(xb, 8 * g + i) * before] + [lines[p][i + 1] for p in range(4)] + [load(xa, 8 * g + i) * after]
                for p in range(4):
                    t = turned[p]
                    around = line[p] + line[p + 2]
                    value = stencil(line[p + 1], t[i + 1], t[i], t[i + 2], around, has_next, x + p, 8 * g + i)
                    if deep == BOX:
                        dest, slot = at(p, i)
                        out_ref[dest, :, pl.ds(slot, 128)] = value.astype(bf16)
                    else:
                        held[:, p * 1024 + i * 128 : p * 1024 + (i + 1) * 128] = value * live
            if deep == BOX:
                return

            def kept(p, i):
                return held[:, p * 1024 + i * 128 : p * 1024 + (i + 1) * 128]

            for i in range(8):
                for p in range(deep // 16):
                    if deep == 32:
                        value = kept(2 * p, i) + pltpu.roll(kept(2 * p + 1, i), 32, 1)
                    else:
                        piece = (z >= 16 * p) & (z < 16 * p + 16)
                        value = kept(p, i) + pltpu.roll(jnp.where(piece, kept(3, i), 0.0), 48 - 16 * p, 1)
                    dest, slot = at(p, i)
                    out_ref[dest, :, pl.ds(slot, 128)] = value.astype(bf16)

        each_part(size, per_dest, deep, part, ready)

    for deep in (32, 48, 64):
        some(deep)


def unpack_kernel(meta, in_ref, out_ref):
    size = box_size(meta)
    sx, sy, sz = size
    per_dest = (sx * sy * sz) // (PEERS * 128)
    lane = lax.broadcasted_iota(jnp.int32, (8, 128), 1)
    z = lane % BOX

    def put(x, i, value):
        out_ref[:, pl.ds(aligned(x * PLANE + i * 128), 128)] = value.astype(bf16)

    @pl.when(per_dest == VOLUMES[-1])
    def _():
        def quad(q, carry):
            for i in range(32):
                for p in range(4):
                    dest, slot = full_place(q, p, i)
                    put(4 * q + p, i, in_ref[dest, :, slot : slot + 128])
            return carry

        lax.fori_loop(0, BOX // 4, quad, 0)

    @pl.when(per_dest < VOLUMES[-1])
    def _():
        def clear(i, carry):
            out_ref[:, pl.ds(aligned(i * PLANE), PLANE)] = jnp.zeros((8, PLANE), bf16)
            return carry

        lax.fori_loop(0, BOX, clear, 0)

    def some(deep):
        live = (z < deep).astype(f32)
        gap = (z >= deep).astype(f32)

        def part(x, g, at):
            for i in range(8):
                row = 8 * g + i
                values = []
                for p in range(deep // 16):
                    dest, slot = at(p, i)
                    values.append(in_ref[dest, :, pl.ds(slot, 128)])
                if deep == 64:
                    for p in range(4):
                        put(x + p, row, values[p])
                    continue
                values = [value.astype(f32) for value in values]
                if deep == 32:
                    for p in range(2):
                        put(x + 2 * p, row, values[p] * live)
                        put(x + 2 * p + 1, row, pltpu.roll(values[p], 96, 1) * live)
                else:
                    for p in range(3):
                        put(x + p, row, values[p] * live)
                    rest = [pltpu.roll(values[p] * gap, 80 + 16 * p, 1) for p in range(3)]
                    put(x + 3, row, rest[0] + rest[1] + rest[2])

        each_part(size, per_dest, deep, part)

    for deep in (32, 48, 64):
        some(deep)


def gram_kernel(rows_ref, out_ref, blocks, arrived):
    copies = []
    for i in range(OWN):
        part = rows_ref.at[:, i * EXTRA : (i + 1) * EXTRA]
        copies.append(pltpu.make_async_copy(part, blocks.at[i], arrived.at[i]))
        copies[-1].start()
    total = jnp.zeros((NB, NB), f32)
    for i in range(OWN):
        copies[i].wait()
        block = blocks[i]
        total = total + lax.dot_general(block, block, (((1,), (1,)), ((), ())), preferred_element_type=f32)
    out_ref[...] = total


def halves(value):
    head = value.astype(bf16)
    return head, (value - head.astype(f32)).astype(bf16)


def product(left, right):
    dot = functools.partial(jnp.dot, preferred_element_type=f32)
    return dot(left[0], right[0]) + (dot(left[0], right[1]) + dot(left[1], right[0]))


def newton_kernel(gram_ref, out_ref):
    gram = gram_ref[...] * (1.0 / CELLS)
    frobenius = jnp.sqrt(jnp.sum(gram * gram, keepdims=True) + epsilon)
    row = lax.broadcasted_iota(jnp.int32, (NB, NB), 0)
    column = lax.broadcasted_iota(jnp.int32, (NB, NB), 1)
    three = jnp.where(row == column, 1.5, 0.0)
    square = gram / frobenius
    step = halves(three - 0.5 * square)
    inverse = step
    square = halves(product(halves(square), step))
    for sweep in range(1, NS_ITERS):
        step = halves(three - 0.5 * product(inverse, square))
        if sweep < NS_ITERS - 1:
            square = halves(product(square, step))
        inverse = product(step, inverse)
        if sweep < NS_ITERS - 1:
            inverse = halves(inverse)
    out_ref[...] = (inverse / jnp.sqrt(frobenius)).T.astype(bf16)


def fresh_kernel(coeff_ref, rows_ref, occ_ref, out_ref, blocks, arrived, dens):
    copies = []
    for i in range(OWN):
        part = rows_ref.at[:, i * EXTRA : (i + 1) * EXTRA]
        copies.append(pltpu.make_async_copy(part, blocks.at[i], arrived.at[i]))
        copies[-1].start()
    weight = jnp.broadcast_to(occ_ref[...] * (1.0 / NB), (128, NB)).T[:, 0:1]
    coeff = coeff_ref[...]
    for i in range(OWN):
        copies[i].wait()
        fresh = jnp.dot(coeff, blocks[i], preferred_element_type=f32)
        out_ref[:, i * EXTRA : (i + 1) * EXTRA] = fresh.astype(bf16)
        sums = jnp.sum(weight * fresh * fresh, axis=0, keepdims=True)
        for j in range(8):
            dens[j : j + 1, i * 128 : (i + 1) * 128] = sums[:, j * 128 : (j + 1) * 128]
    block = dens[...].astype(bf16)
    for peer in range(PEERS):
        out_ref[peer * OWN : (peer + 1) * OWN, FULL:] = block


def share_kernel(meta, dens_ref, table_ref, out_ref, box):
    sx, sy, sz = box_size(meta)
    frag, band = meta[PLACE, 0], meta[PLACE, 1]
    groups = sy // 16
    lane = lax.broadcasted_iota(jnp.int32, (8, 128), 1)
    z = lane % BOX
    live = (z < sz).astype(f32)
    box[...] = jnp.zeros((BOX, 32, 128), f32)

    def tile(at):
        return dens_ref[at // 8, :, pl.ds(aligned(at % 8 * 128), 128)].astype(f32)

    def put(x, g, value):
        box[x, pl.ds(pl.multiple_of(g * 8, 8), 8), :] = value

    def parts(deep, body):
        @pl.when(sz == deep)
        def _():
            def outer(q, carry):
                def inner(g, c):
                    body(4 * q, g, [tile((q * groups + g) * (deep // 16) + p) for p in range(deep // 16)])
                    return c

                return lax.fori_loop(0, groups, inner, carry)

            lax.fori_loop(0, sx // 4, outer, 0)

    def whole(x, g, values):
        for p in range(4):
            put(x + p, g, values[p])

    def half(x, g, values):
        for p in range(2):
            put(x + 2 * p, g, values[p] * live)
            put(x + 2 * p + 1, g, pltpu.roll(values[p], 96, 1) * live)

    def most(x, g, values):
        gap = (z >= 48).astype(f32)
        for p in range(3):
            put(x + p, g, values[p] * live)
        rest = [pltpu.roll(values[p] * gap, 80 + 16 * p, 1) for p in range(3)]
        put(x + 3, g, rest[0] + rest[1] + rest[2])

    parts(64, whole)
    parts(32, half)
    parts(48, most)

    ox, oy, _ = box_offset(meta, frag)

    def plane(x):
        inside = ((x >= 0) & (x < sx)).astype(f32)
        return (box[jnp.clip(x, 0, BOX - 1)] * inside).astype(bf16)

    for i in range(4):
        value = plane(4 * band + i - ox)
        for other in range(8):
            out_ref[other, i * 32 : (i + 1) * 32, :] = value
    for other in range(8):
        for j in range(2):
            value = plane(box_offset(meta, other)[0] + 2 * band + j - ox)
            out_ref[other, (4 + j) * 32 : (5 + j) * 32, :] = value

    wide = lax.broadcasted_iota(jnp.int32, (32, 128), 1)
    even = table_ref[pl.ds(oy, 32, stride=2), :]
    odd = table_ref[pl.ds(oy + 1, 32, stride=2), :]
    weights = []
    for k in range(4):
        pick = wide == 4 * band + k
        first = jnp.sum(jnp.where(pick, even, 0.0), axis=1, keepdims=True)
        second = jnp.sum(jnp.where(pick, odd, 0.0), axis=1, keepdims=True)
        weights.append(jnp.where(wide < BOX, first, second))
    low = lane < BOX
    for pair in range(2):
        for part in range(4):
            rows = []
            for half in range(2):
                start = part * 16 + half * 8
                cube = box[start : start + 8]
                sums = []
                for k in (2 * pair, 2 * pair + 1):
                    s = jnp.sum(cube * weights[k][None], axis=1)
                    sums.append(s + pltpu.roll(s, BOX, 1))
                rows.append(jnp.where(low, sums[0], sums[1]))
            value = jnp.concatenate(rows, axis=0).astype(bf16)
            at = 192 + pair * BOX + part * 16
            for other in range(8):
                out_ref[other, at : at + 16, :] = value


def place_kernel(meta, in_ref, patched_ref, placed, target):
    lane = lax.broadcasted_iota(jnp.int32, (32, 128), 1)
    low = lane < BOX
    wide = lax.broadcasted_iota(jnp.int32, (BOX, G), 1)
    line = lax.broadcasted_iota(jnp.int32, (BOX, G), 0)
    for f in range(8):
        _, oy, oz = box_offset(meta, f)
        sign = meta[SIGNS, f].astype(f32)
        for i in range(6):
            value = in_ref[f, i * 32 : (i + 1) * 32, :].astype(f32)
            first = pltpu.roll(jnp.where(low, value, 0.0), oz, 1)
            second = pltpu.roll(jnp.where(low, 0.0, value), (oz + BOX) % G, 1)
            placed[f * BOX : f * BOX + 32, i * G : (i + 1) * G] = first.astype(bf16)
            placed[f * BOX + 32 : (f + 1) * BOX, i * G : (i + 1) * G] = second.astype(bf16)
        lands = oy + 2 * (line % 32) + line // 32
        target[f * BOX : (f + 1) * BOX, :] = jnp.where(wide == lands, sign, 0.0).astype(bf16)
    across = (((0,), (0,)), ((), ()))
    patched_ref[...] = lax.dot_general(target[...], placed[...], across, preferred_element_type=f32)


def solve_kernel(meta, in_ref, table_ref, column_ref, row_ref, out_ref, spread, along, cols, turned):
    frag, band = meta[PLACE, 0], meta[PLACE, 1]
    dot = functools.partial(lax.dot_general, preferred_element_type=f32)
    across = (((0,), (0,)), ((), ()))
    half = lax.broadcasted_iota(jnp.int32, (G, G), 1) < BOX
    for f in range(8):
        ox, _, oz = box_offset(meta, f)
        sign = meta[SIGNS, f].astype(f32)
        part = table_ref[pl.ds(oz, BOX), :]
        part = halves(jnp.concatenate([part, part], axis=0))
        value = in_ref[f, 192:320, :].astype(f32)
        both = jnp.concatenate([jnp.where(half, value, 0.0), jnp.where(half, 0.0, value)], axis=0).astype(bf16)
        both = jnp.dot(both, part[0], preferred_element_type=f32) + jnp.dot(both, part[1], preferred_element_type=f32)
        for parity in range(2):
            for pair in range(2):
                k = 2 * pair + parity
                at = parity * G + pair * BOX
                spread[f * BOX : (f + 1) * BOX, k * G : (k + 1) * G] = both[at : at + BOX, :]
        along[f * BOX : (f + 1) * BOX, :] = table_ref[pl.ds(ox, BOX), :] * sign
    left, right = halves(along[...]), halves(spread[...])
    spectrum = dot(left[0], right[0], across) + (dot(left[0], right[1], across) + dot(left[1], right[0], across))
    table = halves(table_ref[0:G, :])
    ex = column_ref[...]
    ez = row_ref[...]
    spot = lax.broadcasted_iota(jnp.int32, (1, G), 1)
    scaled = []
    for k in range(4):
        ey = jnp.sum(jnp.where(spot == 4 * band + k, ez, 0.0), axis=1, keepdims=True)
        scaled.append(spectrum[:, k * G : (k + 1) * G] * (screening / (ex + ey + ez + screening)))
    solved = product(table, halves(jnp.concatenate(scaled, axis=1)))
    for k in range(4):
        cols[k, 0:G, :] = product(halves(solved[:, k * G : (k + 1) * G]), table)
        cols[k, G : G + BOX, :] = jnp.zeros((BOX, G), f32)
    ox = box_offset(meta, frag)[0]
    for k in range(4):
        for i in range(6):
            part = cols[k, pl.ds(i, 32, stride=4), :] if i < 4 else cols[k, pl.ds(ox + i - 4, 32, stride=2), :]
            turned[i % 3, pl.ds(2 * k + i // 3, 32, stride=8), :] = part
    for i in range(3):
        out_ref[:, i * G : (i + 1) * G] = turned[i].astype(bf16)


def total_kernel(meta, in_ref, local_ref, table_ref, slab_ref, window_ref, columns, rows):
    sx, sy, sz = box_size(meta)
    frag, band = meta[PLACE, 0], meta[PLACE, 1]
    _, oy, oz = box_offset(meta, frag)
    table = halves(table_ref[0:G, :])
    for i in range(3):
        columns[i] = in_ref[:, i * G : (i + 1) * G].astype(f32)

    def total(i):
        part = columns[i % 3, pl.ds(i // 3, G, stride=2), :].astype(bf16)
        hartree = jnp.dot(table[0], part, preferred_element_type=f32) + jnp.dot(table[1], part, preferred_element_type=f32)
        return hartree - local_ref[:, i * G : (i + 1) * G]

    for i in range(4):
        slab_ref[i] = total(i)
    lane = lax.broadcasted_iota(jnp.int32, (32, 128), 1)
    line = lax.broadcasted_iota(jnp.int32, (32, 128), 0)
    live = ((lane % BOX < sz) & (2 * line + lane // BOX < sy)).astype(f32)
    low = lane < BOX
    for j in range(2):
        rows[0:G, :] = total(4 + j)
        rows[G : G + BOX, :] = jnp.zeros((BOX, G), f32)
        even = pltpu.roll(rows[pl.ds(oy, 32, stride=2), :], (G - oz) % G, 1)
        odd = pltpu.roll(rows[pl.ds(oy + 1, 32, stride=2), :], (G + BOX - oz) % G, 1)
        inside = (2 * band + j < sx).astype(f32)
        value = (jnp.where(low, even, odd) * live * inside).astype(bf16)
        for peer in range(PEERS):
            window_ref[peer, j * 32 : (j + 1) * 32, :] = value


def swap(block, axis="band"):
    return lax.all_to_all(block, axis, split_axis=0, concat_axis=0, tiled=True)


def swap_trial(volume, trial):
    lanes = volume * 128
    if lanes == FULL:
        return swap(trial)
    return jnp.pad(swap(trial[:, :, :lanes]), ((0, 0), (0, 0), (0, FULL - lanes)))


def swap_fresh(volume, block):
    lanes = volume * 128
    if lanes == FULL:
        return swap(block)
    tiles = -(-volume // OWN)
    width = tiles * 128
    back = swap(jnp.concatenate([block[:, :, :lanes], block[:, :, FULL : FULL + width]], axis=2))
    dens = back[:, :, lanes:].reshape(PEERS, OWN, tiles, 128).transpose(0, 2, 1, 3).reshape(PEERS, OWN * width)
    dens = jnp.pad(dens[:, :lanes].reshape(PEERS * lanes), (0, CELLS - PEERS * lanes))
    dens = dens.reshape(PEERS, OWN, OWN, 128).transpose(0, 2, 1, 3).reshape(PEERS, OWN, EXTRA)
    return jnp.concatenate([jnp.pad(back[:, :, :lanes], ((0, 0), (0, 0), (0, FULL - lanes))), dens], axis=2)


def body(wave_coeffs, old_potential, occupations, box_sizes, box_offsets, patch_signs):
    fragment = lax.axis_index("frag")
    band_index = lax.axis_index("band")
    here = jnp.where(jnp.arange(8) == 0, fragment, band_index).astype(jnp.int32)
    meta = jnp.concatenate([box_sizes.T, box_offsets.T, patch_signs[None], here[None]], axis=0)
    padded, eigen = sine_table()
    table = jnp.asarray(padded)
    eigen_row, eigen_column = jnp.asarray(eigen[None, :]), jnp.asarray(eigen[:, None])

    trial, kind = pl.pallas_call(
        trial_kernel,
        out_shape=(jax.ShapeDtypeStruct((PEERS, OWN, FULL), bf16), jax.ShapeDtypeStruct((1,), jnp.int32)),
        in_specs=[smem(), pl.BlockSpec(memory_space=pltpu.HBM), pl.BlockSpec(memory_space=pltpu.HBM)],
        out_specs=(vmem(), smem()),
        scratch_shapes=[
            pltpu.VMEM((OWN, 4096), f32),
            pltpu.VMEM((OWN, CELLS), bf16),
            pltpu.VMEM((1, CELLS), f32),
            pltpu.SemaphoreType.DMA((2, BOX // 4)),
        ],
        compiler_params=params(56),
        name="trial",
    )(meta, wave_coeffs[0], old_potential)
    kind = kind[0]
    rows = lax.switch(kind, [functools.partial(swap_trial, v) for v in VOLUMES], trial)
    rows = rows.reshape(NB, FULL)
    partial_value = pl.pallas_call(
        gram_kernel,
        out_shape=jax.ShapeDtypeStruct((NB, NB), f32),
        in_specs=[pl.BlockSpec(memory_space=pltpu.HBM)],
        out_specs=vmem(),
        scratch_shapes=[pltpu.VMEM((OWN, NB, EXTRA), bf16), pltpu.SemaphoreType.DMA((OWN,))],
        compiler_params=params(32),
        name="gram",
    )(rows)
    share = swap(partial_value.reshape(PEERS, OWN, NB)).sum(axis=0)
    gram = swap(jnp.broadcast_to(share[None], (PEERS, OWN, NB))).reshape(NB, NB)
    coeff = pl.pallas_call(
        newton_kernel,
        out_shape=jax.ShapeDtypeStruct((NB, NB), bf16),
        in_specs=[vmem()],
        out_specs=vmem(),
        compiler_params=params(32),
        name="newton",
    )(gram)
    fresh = pl.pallas_call(
        fresh_kernel,
        out_shape=jax.ShapeDtypeStruct((NB, FULL + EXTRA), bf16),
        in_specs=[vmem(), pl.BlockSpec(memory_space=pltpu.HBM), vmem()],
        out_specs=vmem(),
        scratch_shapes=[
            pltpu.VMEM((OWN, NB, EXTRA), bf16),
            pltpu.SemaphoreType.DMA((OWN,)),
            pltpu.VMEM((OWN, EXTRA), f32),
        ],
        compiler_params=params(32),
        name="fresh",
    )(coeff, rows, occupations)
    fresh = fresh.reshape(PEERS, OWN, FULL + EXTRA)
    back = lax.switch(kind, [functools.partial(swap_fresh, v) for v in VOLUMES], fresh)
    shared = pl.pallas_call(
        share_kernel,
        out_shape=jax.ShapeDtypeStruct((8, 320, 128), bf16),
        grid=(1,),
        in_specs=[
            smem(),
            pl.BlockSpec((PEERS, OWN, EXTRA), lambda i: (0, 0, FULL // EXTRA)),
            pl.BlockSpec((G + BOX, G), lambda i: (0, 0)),
        ],
        out_specs=pl.BlockSpec((8, 320, 128), lambda i: (0, 0, 0)),
        scratch_shapes=[pltpu.VMEM((BOX, 32, 128), f32)],
        compiler_params=params(32),
        name="share",
    )(meta, back, table)
    parts = swap(shared, "frag")
    columns = pl.pallas_call(
        solve_kernel,
        out_shape=jax.ShapeDtypeStruct((2 * G, 3 * G), bf16),
        in_specs=[smem(), vmem(), vmem(), vmem(), vmem()],
        out_specs=vmem(),
        scratch_shapes=[
            pltpu.VMEM((8 * BOX, 4 * G), f32),
            pltpu.VMEM((8 * BOX, G), f32),
            pltpu.VMEM((4, G + BOX, G), f32),
            pltpu.VMEM((3, 2 * G, G), f32),
        ],
        compiler_params=params(32),
        name="solve",
    )(meta, parts, table, eigen_column, eigen_row)
    patched = pl.pallas_call(
        place_kernel,
        out_shape=jax.ShapeDtypeStruct((G, 6 * G), f32),
        in_specs=[smem(), vmem()],
        out_specs=vmem(),
        scratch_shapes=[pltpu.VMEM((8 * BOX, 6 * G), bf16), pltpu.VMEM((8 * BOX, G), bf16)],
        compiler_params=params(32),
        cost_estimate=pl.CostEstimate(flops=2 * 8 * BOX * 6 * G * G, bytes_accessed=2**20, transcendentals=0),
        name="place",
    )(meta, parts)
    columns = swap(columns.reshape(PEERS, 8, 3 * G)).reshape(2 * G, 3 * G)
    local = local_factor * jnp.cbrt(jnp.maximum(patched, 0.0))
    total_potential, window = pl.pallas_call(
        total_kernel,
        out_shape=(jax.ShapeDtypeStruct((4, G, G), f32), jax.ShapeDtypeStruct((PEERS, 64, 128), bf16)),
        in_specs=[smem(), vmem(), vmem(), vmem()],
        out_specs=(vmem(), vmem()),
        scratch_shapes=[pltpu.VMEM((3, 2 * G, G), f32), pltpu.VMEM((G + BOX, G), f32)],
        compiler_params=params(32),
        name="total",
    )(meta, columns, local, table)
    window = swap(window)
    waves_out = pl.pallas_call(
        unpack_kernel,
        out_shape=jax.ShapeDtypeStruct((OWN, CELLS), bf16),
        in_specs=[smem(), vmem()],
        out_specs=vmem(),
        compiler_params=params(32),
        name="unpack",
    )(meta, back)
    box_potential = window.astype(f32).reshape(1, CELLS)
    return (waves_out[None], box_potential, total_potential)


def solution(mesh):
    placed = (P("frag", "band", None), P("frag", None), P("frag", None), P(), P(), P())
    return jax.shard_map(
        body,
        mesh=mesh,
        in_specs=placed,
        out_specs=(P("frag", "band", None), P("frag", None), P("band", None, None)),
        check_vma=False,
    )
```

```python
import functools

import jax
import jax.numpy as jnp
import numpy as np
from jax import lax
from jax.experimental import pallas as pl
from jax.experimental.pallas import tpu as pltpu
from jax.sharding import PartitionSpec as P

NB = 256
BOX = 64
G = 128
NS_ITERS = 8
CELLS = BOX**3
PLANE = BOX * BOX
PEERS = 32
OWN = NB // PEERS
FULL = CELLS // PEERS
EXTRA = FULL // OWN
SIZES, OFFSETS, SIGNS, PLACE = 0, 3, 6, 7
VOLUMES = (8, 12, 16, 18, 24, 27, 32, 36, 48, 64)

step_size = 0.1
screening = 0.5
local_factor = 0.75
epsilon = 1e-06
f32 = jnp.float32
bf16 = jnp.bfloat16


def sine_table():
    index = np.arange(G, dtype=np.float64) + 1.0
    table = np.sqrt(2.0 / (G + 1)) * np.sin(np.pi * index[:, None] * index[None, :] / (G + 1))
    eigen = 2.0 - 2.0 * np.cos(np.pi * index / (G + 1))
    padded = np.zeros((G + BOX, G), np.float32)
    padded[:G] = table
    return padded, eigen.astype(np.float32)


def aligned(offset):
    return pl.multiple_of(offset, 128)


def vmem():
    return pl.BlockSpec(memory_space=pltpu.VMEM)


def smem():
    return pl.BlockSpec(memory_space=pltpu.SMEM)


def box_size(meta):
    f = meta[PLACE, 0]
    return meta[SIZES, f], meta[SIZES + 1, f], meta[SIZES + 2, f]


def box_offset(meta, f):
    return meta[OFFSETS, f], meta[OFFSETS + 1, f], meta[OFFSETS + 2, f]


def params(mib):
    return pltpu.CompilerParams(vmem_limit_bytes=mib * 1024 * 1024)


def runs(total, run, per_dest, carry):
    dest, slot = carry
    places = []
    for _ in range(total // run):
        places.append((dest, slot))
        slot = slot + run
        wrap = slot == per_dest
        dest, slot = jnp.where(wrap, dest + 1, dest), jnp.where(wrap, 0, slot)
    return places, (dest, slot)


def each_part(size, per_dest, deep, body, ready=None):
    sx, sy, sz = size
    run = {64: 4, 32: 2, 48: 1}[deep]

    @pl.when((sz == deep) & (per_dest < VOLUMES[-1]))
    def _():
        def quad(q, carry):
            if ready is not None:
                ready(q + 1)

            def part(g, place):
                places, place = runs(deep // 2, run, per_dest, place)

                def at(plane, i):
                    dest, slot = places[(plane * 8 + i) // run]
                    return dest, aligned((slot + i % run) * 128)

                body(4 * q, g, at)
                return place

            return lax.fori_loop(0, sy // 16, part, carry)

        lax.fori_loop(0, sx // 4, quad, (jnp.int32(0), jnp.int32(0)))


def full_place(q, plane, i):
    flat = i // 8 * 32 + plane * 8 + i % 8
    return 2 * q + flat // 64, flat % 64 * 128


def trial_kernel(meta, wave_in, pot_in, out_ref, kind_ref, held, wave_ref, pot_ref, arrived):
    size = box_size(meta)
    sx, sy, sz = size
    per_dest = (sx * sy * sz) // (PEERS * 128)
    kind = jnp.int32(0)
    for volume in VOLUMES:
        kind = kind + (volume < per_dest).astype(jnp.int32)
    kind_ref[0] = kind
    quads = sx // 4

    def fetch(q):
        lanes = pl.ds(aligned(q * 4 * PLANE), 4 * PLANE)
        wave = pltpu.make_async_copy(wave_in.at[:, lanes], wave_ref.at[:, lanes], arrived.at[0, q])
        return wave, pltpu.make_async_copy(pot_in.at[:, lanes], pot_ref.at[:, lanes], arrived.at[1, q])

    def begin(q, carry):
        for copy in fetch(q):
            copy.start()
        return carry

    def ready(q):
        @pl.when(q < quads)
        def _():
            for copy in fetch(q):
                copy.wait()

    lax.fori_loop(0, quads, begin, 0)
    ready(0)
    lane = lax.broadcasted_iota(jnp.int32, (8, 128), 1)
    z = lane % BOX
    low = lane < BOX
    has_last = (z > 0).astype(f32)
    zero = jnp.zeros((8, 128), f32)

    def load(x, i):
        return wave_ref[:, pl.ds(aligned(x * PLANE + i * 128), 128)].astype(f32)

    def edges(x):
        before = jnp.where(x > 0, 1.0, 0.0)
        after = jnp.where(x + 4 < sx, 1.0, 0.0)
        return before, after, jnp.maximum(x - 1, 0), jnp.minimum(x + 4, sx - 1)

    def stencil(c, turned, last_turned, next_turned, around, has_next, x, i):
        beside = turned + jnp.where(low, last_turned, next_turned)
        beside = beside + (pltpu.roll(c, 127, 1) * has_next + pltpu.roll(c, 1, 1) * has_last)
        beside = beside + around
        pot = pot_ref[:, pl.ds(aligned(x * PLANE + i * 128), 128)]
        return c * ((1.0 - 3.0 * step_size) - step_size * pot) + (0.5 * step_size) * beside

    @pl.when(per_dest == VOLUMES[-1])
    def _():
        has_next = (z < BOX - 1).astype(f32)

        def quad(q, carry):
            ready(q + 1)
            x = 4 * q
            before, after, xb, xa = edges(x)
            last_turned, here = [zero] * 4, [load(x + p, 0) for p in range(4)]
            turned = [pltpu.roll(c, BOX, 1) for c in here]
            for i in range(32):
                ahead = [load(x + p, i + 1) for p in range(4)] if i < 31 else [zero] * 4
                ahead_turned = [pltpu.roll(c, BOX, 1) for c in ahead] if i < 31 else [zero] * 4
                line = [load(xb, i) * before] + here + [load(xa, i) * after]
                for p in range(4):
                    around = line[p] + line[p + 2]
                    value = stencil(here[p], turned[p], last_turned[p], ahead_turned[p], around, has_next, x + p, i)
                    dest, slot = full_place(q, p, i)
                    out_ref[dest, :, slot : slot + 128] = value.astype(bf16)
                here, last_turned, turned = ahead, turned, ahead_turned
            return carry

        lax.fori_loop(0, BOX // 4, quad, 0)

    def some(deep):
        live = (z < deep).astype(f32)
        has_next = (z < deep - 1).astype(f32)

        def part(x, g, at):
            before, after, xb, xa = edges(x)
            top = jnp.where(g > 0, 1.0, 0.0)
            bottom = jnp.where(16 * g + 16 < sy, 1.0, 0.0)
            first, last = jnp.maximum(8 * g - 1, 0), jnp.minimum(8 * g + 8, 31)
            lines = []
            for p in range(4):
                inner = [load(x + p, 8 * g + i) for i in range(8)]
                lines.append([load(x + p, first) * top] + inner + [load(x + p, last) * bottom])
            turned = [[pltpu.roll(c, BOX, 1) for c in line] for line in lines]
            for i in range(8):
                line = [load(xb, 8 * g + i) * before] + [lines[p][i + 1] for p in range(4)] + [load(xa, 8 * g + i) * after]
                for p in range(4):
                    t = turned[p]
                    around = line[p] + line[p + 2]
                    value = stencil(line[p + 1], t[i + 1], t[i], t[i + 2], around, has_next, x + p, 8 * g + i)
                    if deep == BOX:
                        dest, slot = at(p, i)
                        out_ref[dest, :, pl.ds(slot, 128)] = value.astype(bf16)
                    else:
                        held[:, p * 1024 + i * 128 : p * 1024 + (i + 1) * 128] = value * live
            if deep == BOX:
                return

            def kept(p, i):
                return held[:, p * 1024 + i * 128 : p * 1024 + (i + 1) * 128]

            for i in range(8):
                for p in range(deep // 16):
                    if deep == 32:
                        value = kept(2 * p, i) + pltpu.roll(kept(2 * p + 1, i), 32, 1)
                    else:
                        piece = (z >= 16 * p) & (z < 16 * p + 16)
                        value = kept(p, i) + pltpu.roll(jnp.where(piece, kept(3, i), 0.0), 48 - 16 * p, 1)
                    dest, slot = at(p, i)
                    out_ref[dest, :, pl.ds(slot, 128)] = value.astype(bf16)

        each_part(size, per_dest, deep, part, ready)

    for deep in (32, 48, 64):
        some(deep)


def unpack_kernel(meta, in_ref, out_ref):
    size = box_size(meta)
    sx, sy, sz = size
    per_dest = (sx * sy * sz) // (PEERS * 128)
    lane = lax.broadcasted_iota(jnp.int32, (8, 128), 1)
    z = lane % BOX

    def put(x, i, value):
        out_ref[:, pl.ds(aligned(x * PLANE + i * 128), 128)] = value.astype(bf16)

    @pl.when(per_dest == VOLUMES[-1])
    def _():
        def quad(q, carry):
            for i in range(32):
                for p in range(4):
                    dest, slot = full_place(q, p, i)
                    put(4 * q + p, i, in_ref[dest, :, slot : slot + 128])
            return carry

        lax.fori_loop(0, BOX // 4, quad, 0)

    @pl.when(per_dest < VOLUMES[-1])
    def _():
        def clear(i, carry):
            out_ref[:, pl.ds(aligned(i * PLANE), PLANE)] = jnp.zeros((8, PLANE), bf16)
            return carry

        lax.fori_loop(0, BOX, clear, 0)

    def some(deep):
        live = (z < deep).astype(f32)
        gap = (z >= deep).astype(f32)

        def part(x, g, at):
            for i in range(8):
                row = 8 * g + i
                values = []
                for p in range(deep // 16):
                    dest, slot = at(p, i)
                    values.append(in_ref[dest, :, pl.ds(slot, 128)])
                if deep == 64:
                    for p in range(4):
                        put(x + p, row, values[p])
                    continue
                values = [value.astype(f32) for value in values]
                if deep == 32:
                    for p in range(2):
                        put(x + 2 * p, row, values[p] * live)
                        put(x + 2 * p + 1, row, pltpu.roll(values[p], 96, 1) * live)
                else:
                    for p in range(3):
                        put(x + p, row, values[p] * live)
                    rest = [pltpu.roll(values[p] * gap, 80 + 16 * p, 1) for p in range(3)]
                    put(x + 3, row, rest[0] + rest[1] + rest[2])

        each_part(size, per_dest, deep, part)

    for deep in (32, 48, 64):
        some(deep)


def gram_kernel(rows_ref, out_ref):
    total = jnp.zeros((NB, NB), f32)
    for i in range(OWN):
        block = rows_ref[:, i * EXTRA : (i + 1) * EXTRA]
        total = total + lax.dot_general(block, block, (((1,), (1,)), ((), ())), preferred_element_type=f32)
    out_ref[...] = total


def halves(value):
    head = value.astype(bf16)
    return head, (value - head.astype(f32)).astype(bf16)


def product(left, right):
    dot = functools.partial(jnp.dot, preferred_element_type=f32)
    return dot(left[0], right[0]) + (dot(left[0], right[1]) + dot(left[1], right[0]))


def newton_kernel(gram_ref, out_ref):
    gram = gram_ref[...] * (1.0 / CELLS)
    frobenius = jnp.sqrt(jnp.sum(gram * gram, keepdims=True) + epsilon)
    row = lax.broadcasted_iota(jnp.int32, (NB, NB), 0)
    column = lax.broadcasted_iota(jnp.int32, (NB, NB), 1)
    three = jnp.where(row == column, 1.5, 0.0)
    square = gram / frobenius
    step = halves(three - 0.5 * square)
    inverse = step
    square = halves(product(halves(square), step))
    for sweep in range(1, NS_ITERS):
        step = halves(three - 0.5 * product(inverse, square))
        if sweep < NS_ITERS - 1:
            square = halves(product(square, step))
        inverse = product(step, inverse)
        if sweep < NS_ITERS - 1:
            inverse = halves(inverse)
    out_ref[...] = (inverse / jnp.sqrt(frobenius)).T.astype(bf16)


def fresh_kernel(coeff_ref, rows_ref, occ_ref, out_ref, dens):
    weight = jnp.broadcast_to(occ_ref[...] * (1.0 / NB), (128, NB)).T[:, 0:1]
    coeff = coeff_ref[...]
    for i in range(OWN):
        fresh = jnp.dot(coeff, rows_ref[:, i * EXTRA : (i + 1) * EXTRA], preferred_element_type=f32)
        out_ref[:, i * EXTRA : (i + 1) * EXTRA] = fresh.astype(bf16)
        sums = jnp.sum(weight * fresh * fresh, axis=0, keepdims=True)
        for j in range(8):
            dens[j : j + 1, i * 128 : (i + 1) * 128] = sums[:, j * 128 : (j + 1) * 128]
    block = dens[...].astype(bf16)
    for peer in range(PEERS):
        out_ref[peer * OWN : (peer + 1) * OWN, FULL:] = block


def share_kernel(meta, dens_ref, table_ref, out_ref, box):
    sx, sy, sz = box_size(meta)
    frag, band = meta[PLACE, 0], meta[PLACE, 1]
    groups = sy // 16
    lane = lax.broadcasted_iota(jnp.int32, (8, 128), 1)
    z = lane % BOX
    live = (z < sz).astype(f32)
    box[...] = jnp.zeros((BOX, 32, 128), f32)

    def tile(at):
        return dens_ref[at // 8, :, pl.ds(aligned(at % 8 * 128), 128)].astype(f32)

    def put(x, g, value):
        box[x, pl.ds(pl.multiple_of(g * 8, 8), 8), :] = value

    def parts(deep, body):
        @pl.when(sz == deep)
        def _():
            def outer(q, carry):
                def inner(g, c):
                    body(4 * q, g, [tile((q * groups + g) * (deep // 16) + p) for p in range(deep // 16)])
                    return c

                return lax.fori_loop(0, groups, inner, carry)

            lax.fori_loop(0, sx // 4, outer, 0)

    def whole(x, g, values):
        for p in range(4):
            put(x + p, g, values[p])

    def half(x, g, values):
        for p in range(2):
            put(x + 2 * p, g, values[p] * live)
            put(x + 2 * p + 1, g, pltpu.roll(values[p], 96, 1) * live)

    def most(x, g, values):
        gap = (z >= 48).astype(f32)
        for p in range(3):
            put(x + p, g, values[p] * live)
        rest = [pltpu.roll(values[p] * gap, 80 + 16 * p, 1) for p in range(3)]
        put(x + 3, g, rest[0] + rest[1] + rest[2])

    parts(64, whole)
    parts(32, half)
    parts(48, most)

    ox, oy, _ = box_offset(meta, frag)

    def plane(x):
        inside = ((x >= 0) & (x < sx)).astype(f32)
        return (box[jnp.clip(x, 0, BOX - 1)] * inside).astype(bf16)

    for i in range(4):
        value = plane(4 * band + i - ox)
        for other in range(8):
            out_ref[other, i * 32 : (i + 1) * 32, :] = value
    for other in range(8):
        for j in range(2):
            value = plane(box_offset(meta, other)[0] + 2 * band + j - ox)
            out_ref[other, (4 + j) * 32 : (5 + j) * 32, :] = value

    wide = lax.broadcasted_iota(jnp.int32, (32, 128), 1)
    even = table_ref[pl.ds(oy, 32, stride=2), :]
    odd = table_ref[pl.ds(oy + 1, 32, stride=2), :]
    weights = []
    for k in range(4):
        pick = wide == 4 * band + k
        first = jnp.sum(jnp.where(pick, even, 0.0), axis=1, keepdims=True)
        second = jnp.sum(jnp.where(pick, odd, 0.0), axis=1, keepdims=True)
        weights.append(jnp.where(wide < BOX, first, second))
    low = lane < BOX
    for pair in range(2):
        for part in range(4):
            rows = []
            for half in range(2):
                start = part * 16 + half * 8
                cube = box[start : start + 8]
                sums = []
                for k in (2 * pair, 2 * pair + 1):
                    s = jnp.sum(cube * weights[k][None], axis=1)
                    sums.append(s + pltpu.roll(s, BOX, 1))
                rows.append(jnp.where(low, sums[0], sums[1]))
            value = jnp.concatenate(rows, axis=0).astype(bf16)
            at = 192 + pair * BOX + part * 16
            for other in range(8):
                out_ref[other, at : at + 16, :] = value


def place_kernel(meta, in_ref, patched_ref, placed, target):
    lane = lax.broadcasted_iota(jnp.int32, (32, 128), 1)
    low = lane < BOX
    wide = lax.broadcasted_iota(jnp.int32, (BOX, G), 1)
    line = lax.broadcasted_iota(jnp.int32, (BOX, G), 0)
    for f in range(8):
        _, oy, oz = box_offset(meta, f)
        sign = meta[SIGNS, f].astype(f32)
        for i in range(6):
            value = in_ref[f, i * 32 : (i + 1) * 32, :].astype(f32)
            first = pltpu.roll(jnp.where(low, value, 0.0), oz, 1)
            second = pltpu.roll(jnp.where(low, 0.0, value), (oz + BOX) % G, 1)
            placed[f * BOX : f * BOX + 32, i * G : (i + 1) * G] = first.astype(bf16)
            placed[f * BOX + 32 : (f + 1) * BOX, i * G : (i + 1) * G] = second.astype(bf16)
        lands = oy + 2 * (line % 32) + line // 32
        target[f * BOX : (f + 1) * BOX, :] = jnp.where(wide == lands, sign, 0.0).astype(bf16)
    across = (((0,), (0,)), ((), ()))
    patched_ref[...] = lax.dot_general(target[...], placed[...], across, preferred_element_type=f32)


def solve_kernel(meta, in_ref, table_ref, column_ref, row_ref, out_ref, spread, along, cols, turned):
    frag, band = meta[PLACE, 0], meta[PLACE, 1]
    dot = functools.partial(lax.dot_general, preferred_element_type=f32)
    across = (((0,), (0,)), ((), ()))
    half = lax.broadcasted_iota(jnp.int32, (G, G), 1) < BOX
    for f in range(8):
        ox, _, oz = box_offset(meta, f)
        sign = meta[SIGNS, f].astype(f32)
        part = table_ref[pl.ds(oz, BOX), :]
        part = halves(jnp.concatenate([part, part], axis=0))
        value = in_ref[f, 192:320, :].astype(f32)
        both = jnp.concatenate([jnp.where(half, value, 0.0), jnp.where(half, 0.0, value)], axis=0).astype(bf16)
        both = jnp.dot(both, part[0], preferred_element_type=f32) + jnp.dot(both, part[1], preferred_element_type=f32)
        for parity in range(2):
            for pair in range(2):
                k = 2 * pair + parity
                at = parity * G + pair * BOX
                spread[f * BOX : (f + 1) * BOX, k * G : (k + 1) * G] = both[at : at + BOX, :]
        along[f * BOX : (f + 1) * BOX, :] = table_ref[pl.ds(ox, BOX), :] * sign
    left, right = halves(along[...]), halves(spread[...])
    spectrum = dot(left[0], right[0], across) + (dot(left[0], right[1], across) + dot(left[1], right[0], across))
    table = halves(table_ref[0:G, :])
    ex = column_ref[...]
    ez = row_ref[...]
    spot = lax.broadcasted_iota(jnp.int32, (1, G), 1)
    scaled = []
    for k in range(4):
        ey = jnp.sum(jnp.where(spot == 4 * band + k, ez, 0.0), axis=1, keepdims=True)
        scaled.append(spectrum[:, k * G : (k + 1) * G] * (screening / (ex + ey + ez + screening)))
    solved = product(table, halves(jnp.concatenate(scaled, axis=1)))
    for k in range(4):
        cols[k, 0:G, :] = product(halves(solved[:, k * G : (k + 1) * G]), table)
        cols[k, G : G + BOX, :] = jnp.zeros((BOX, G), f32)
    ox = box_offset(meta, frag)[0]
    for k in range(4):
        for i in range(6):
            part = cols[k, pl.ds(i, 32, stride=4), :] if i < 4 else cols[k, pl.ds(ox + i - 4, 32, stride=2), :]
            turned[i % 3, pl.ds(2 * k + i // 3, 32, stride=8), :] = part
    for i in range(3):
        out_ref[:, i * G : (i + 1) * G] = turned[i].astype(bf16)


def total_kernel(meta, in_ref, local_ref, table_ref, slab_ref, window_ref, columns, rows):
    sx, sy, sz = box_size(meta)
    frag, band = meta[PLACE, 0], meta[PLACE, 1]
    _, oy, oz = box_offset(meta, frag)
    table = halves(table_ref[0:G, :])
    for i in range(3):
        columns[i] = in_ref[:, i * G : (i + 1) * G].astype(f32)

    def total(i):
        part = columns[i % 3, pl.ds(i // 3, G, stride=2), :].astype(bf16)
        hartree = jnp.dot(table[0], part, preferred_element_type=f32) + jnp.dot(table[1], part, preferred_element_type=f32)
        return hartree - local_ref[:, i * G : (i + 1) * G]

    for i in range(4):
        slab_ref[i] = total(i)
    lane = lax.broadcasted_iota(jnp.int32, (32, 128), 1)
    line = lax.broadcasted_iota(jnp.int32, (32, 128), 0)
    live = ((lane % BOX < sz) & (2 * line + lane // BOX < sy)).astype(f32)
    low = lane < BOX
    for j in range(2):
        rows[0:G, :] = total(4 + j)
        rows[G : G + BOX, :] = jnp.zeros((BOX, G), f32)
        even = pltpu.roll(rows[pl.ds(oy, 32, stride=2), :], (G - oz) % G, 1)
        odd = pltpu.roll(rows[pl.ds(oy + 1, 32, stride=2), :], (G + BOX - oz) % G, 1)
        inside = (2 * band + j < sx).astype(f32)
        value = (jnp.where(low, even, odd) * live * inside).astype(bf16)
        for peer in range(PEERS):
            window_ref[peer, j * 32 : (j + 1) * 32, :] = value


def swap(block, axis="band"):
    return lax.all_to_all(block, axis, split_axis=0, concat_axis=0, tiled=True)


def swap_trial(volume, trial):
    lanes = volume * 128
    if lanes == FULL:
        return swap(trial)
    return jnp.pad(swap(trial[:, :, :lanes]), ((0, 0), (0, 0), (0, FULL - lanes)))


def swap_fresh(volume, block):
    lanes = volume * 128
    if lanes == FULL:
        return swap(block)
    tiles = -(-volume // OWN)
    width = tiles * 128
    back = swap(jnp.concatenate([block[:, :, :lanes], block[:, :, FULL : FULL + width]], axis=2))
    dens = back[:, :, lanes:].reshape(PEERS, OWN, tiles, 128).transpose(0, 2, 1, 3).reshape(PEERS, OWN * width)
    dens = jnp.pad(dens[:, :lanes].reshape(PEERS * lanes), (0, CELLS - PEERS * lanes))
    dens = dens.reshape(PEERS, OWN, OWN, 128).transpose(0, 2, 1, 3).reshape(PEERS, OWN, EXTRA)
    return jnp.concatenate([jnp.pad(back[:, :, :lanes], ((0, 0), (0, 0), (0, FULL - lanes))), dens], axis=2)


def body(wave_coeffs, old_potential, occupations, box_sizes, box_offsets, patch_signs):
    fragment = lax.axis_index("frag")
    band_index = lax.axis_index("band")
    here = jnp.where(jnp.arange(8) == 0, fragment, band_index).astype(jnp.int32)
    meta = jnp.concatenate([box_sizes.T, box_offsets.T, patch_signs[None], here[None]], axis=0)
    padded, eigen = sine_table()
    table = jnp.asarray(padded)
    eigen_row, eigen_column = jnp.asarray(eigen[None, :]), jnp.asarray(eigen[:, None])

    trial, kind = pl.pallas_call(
        trial_kernel,
        out_shape=(jax.ShapeDtypeStruct((PEERS, OWN, FULL), bf16), jax.ShapeDtypeStruct((1,), jnp.int32)),
        in_specs=[smem(), pl.BlockSpec(memory_space=pltpu.HBM), pl.BlockSpec(memory_space=pltpu.HBM)],
        out_specs=(vmem(), smem()),
        scratch_shapes=[
            pltpu.VMEM((OWN, 4096), f32),
            pltpu.VMEM((OWN, CELLS), bf16),
            pltpu.VMEM((1, CELLS), f32),
            pltpu.SemaphoreType.DMA((2, BOX // 4)),
        ],
        compiler_params=params(56),
        name="trial",
    )(meta, wave_coeffs[0], old_potential)
    kind = kind[0]
    rows = lax.switch(kind, [functools.partial(swap_trial, v) for v in VOLUMES], trial)
    rows = rows.reshape(NB, FULL)
    partial_value = pl.pallas_call(
        gram_kernel,
        out_shape=jax.ShapeDtypeStruct((NB, NB), f32),
        in_specs=[vmem()],
        out_specs=vmem(),
        compiler_params=params(16),
        name="gram",
    )(rows)
    share = swap(partial_value.reshape(PEERS, OWN, NB)).sum(axis=0)
    gram = swap(jnp.broadcast_to(share[None], (PEERS, OWN, NB))).reshape(NB, NB)
    coeff = pl.pallas_call(
        newton_kernel,
        out_shape=jax.ShapeDtypeStruct((NB, NB), bf16),
        in_specs=[vmem()],
        out_specs=vmem(),
        compiler_params=params(16),
        name="newton",
    )(gram)
    fresh = pl.pallas_call(
        fresh_kernel,
        out_shape=jax.ShapeDtypeStruct((NB, FULL + EXTRA), bf16),
        in_specs=[vmem(), vmem(), vmem()],
        out_specs=vmem(),
        scratch_shapes=[pltpu.VMEM((OWN, EXTRA), f32)],
        compiler_params=params(16),
        name="fresh",
    )(coeff, rows, occupations)
    fresh = fresh.reshape(PEERS, OWN, FULL + EXTRA)
    back = lax.switch(kind, [functools.partial(swap_fresh, v) for v in VOLUMES], fresh)
    shared = pl.pallas_call(
        share_kernel,
        out_shape=jax.ShapeDtypeStruct((8, 320, 128), bf16),
        grid=(1,),
        in_specs=[
            smem(),
            pl.BlockSpec((PEERS, OWN, EXTRA), lambda i: (0, 0, FULL // EXTRA)),
            pl.BlockSpec((G + BOX, G), lambda i: (0, 0)),
        ],
        out_specs=pl.BlockSpec((8, 320, 128), lambda i: (0, 0, 0)),
        scratch_shapes=[pltpu.VMEM((BOX, 32, 128), f32)],
        compiler_params=params(32),
        name="share",
    )(meta, back, table)
    parts = swap(shared, "frag")
    columns = pl.pallas_call(
        solve_kernel,
        out_shape=jax.ShapeDtypeStruct((2 * G, 3 * G), bf16),
        in_specs=[smem(), vmem(), vmem(), vmem(), vmem()],
        out_specs=vmem(),
        scratch_shapes=[
            pltpu.VMEM((8 * BOX, 4 * G), f32),
            pltpu.VMEM((8 * BOX, G), f32),
            pltpu.VMEM((4, G + BOX, G), f32),
            pltpu.VMEM((3, 2 * G, G), f32),
        ],
        compiler_params=params(32),
        name="solve",
    )(meta, parts, table, eigen_column, eigen_row)
    patched = pl.pallas_call(
        place_kernel,
        out_shape=jax.ShapeDtypeStruct((G, 6 * G), f32),
        in_specs=[smem(), vmem()],
        out_specs=vmem(),
        scratch_shapes=[pltpu.VMEM((8 * BOX, 6 * G), bf16), pltpu.VMEM((8 * BOX, G), bf16)],
        compiler_params=params(32),
        cost_estimate=pl.CostEstimate(flops=2 * 8 * BOX * 6 * G * G, bytes_accessed=2**20, transcendentals=0),
        name="place",
    )(meta, parts)
    columns = swap(columns.reshape(PEERS, 8, 3 * G)).reshape(2 * G, 3 * G)
    local = local_factor * jnp.cbrt(jnp.maximum(patched, 0.0))
    total_potential, window = pl.pallas_call(
        total_kernel,
        out_shape=(jax.ShapeDtypeStruct((4, G, G), f32), jax.ShapeDtypeStruct((PEERS, 64, 128), bf16)),
        in_specs=[smem(), vmem(), vmem(), vmem()],
        out_specs=(vmem(), vmem()),
        scratch_shapes=[pltpu.VMEM((3, 2 * G, G), f32), pltpu.VMEM((G + BOX, G), f32)],
        compiler_params=params(32),
        name="total",
    )(meta, columns, local, table)
    window = swap(window)
    waves_out = pl.pallas_call(
        unpack_kernel,
        out_shape=jax.ShapeDtypeStruct((OWN, CELLS), bf16),
        in_specs=[smem(), vmem()],
        out_specs=vmem(),
        compiler_params=params(32),
        name="unpack",
    )(meta, back)
    box_potential = window.astype(f32).reshape(1, CELLS)
    return (waves_out[None], box_potential, total_potential)


def solution(mesh):
    placed = (P("frag", "band", None), P("frag", None), P("frag", None), P(), P(), P())
    return jax.shard_map(
        body,
        mesh=mesh,
        in_specs=placed,
        out_specs=(P("frag", "band", None), P("frag", None), P("band", None, None)),
        check_vma=False,
    )
```

```python
import functools

import jax
import jax.numpy as jnp
import numpy as np
from jax import lax
from jax.experimental import pallas as pl
from jax.experimental.pallas import tpu as pltpu
from jax.sharding import PartitionSpec as P

NB = 256
BOX = 64
G = 128
NS_ITERS = 8
CELLS = BOX**3
PLANE = BOX * BOX
PEERS = 32
OWN = NB // PEERS
FULL = CELLS // PEERS
EXTRA = FULL // OWN
SIZES, OFFSETS, SIGNS, PLACE = 0, 3, 6, 7
VOLUMES = (8, 12, 16, 18, 24, 27, 32, 36, 48, 64)

step_size = 0.1
screening = 0.5
local_factor = 0.75
epsilon = 1e-06
f32 = jnp.float32
bf16 = jnp.bfloat16


def sine_table():
    index = np.arange(G, dtype=np.float64) + 1.0
    table = np.sqrt(2.0 / (G + 1)) * np.sin(np.pi * index[:, None] * index[None, :] / (G + 1))
    eigen = 2.0 - 2.0 * np.cos(np.pi * index / (G + 1))
    padded = np.zeros((G + BOX, G), np.float32)
    padded[:G] = table
    return padded, eigen.astype(np.float32)


def aligned(offset):
    return pl.multiple_of(offset, 128)


def vmem():
    return pl.BlockSpec(memory_space=pltpu.VMEM)


def smem():
    return pl.BlockSpec(memory_space=pltpu.SMEM)


def box_size(meta):
    f = meta[PLACE, 0]
    return meta[SIZES, f], meta[SIZES + 1, f], meta[SIZES + 2, f]


def box_offset(meta, f):
    return meta[OFFSETS, f], meta[OFFSETS + 1, f], meta[OFFSETS + 2, f]


def params(mib):
    return pltpu.CompilerParams(vmem_limit_bytes=mib * 1024 * 1024)


def runs(total, run, per_dest, carry):
    dest, slot = carry
    places = []
    for _ in range(total // run):
        places.append((dest, slot))
        slot = slot + run
        wrap = slot == per_dest
        dest, slot = jnp.where(wrap, dest + 1, dest), jnp.where(wrap, 0, slot)
    return places, (dest, slot)


def each_part(size, per_dest, deep, body, ready=None):
    sx, sy, sz = size
    run = {64: 4, 32: 2, 48: 1}[deep]

    @pl.when((sz == deep) & (per_dest < VOLUMES[-1]))
    def _():
        def quad(q, carry):
            if ready is not None:
                ready(q + 1)

            def part(g, place):
                places, place = runs(deep // 2, run, per_dest, place)

                def at(plane, i):
                    dest, slot = places[(plane * 8 + i) // run]
                    return dest, aligned((slot + i % run) * 128)

                body(4 * q, g, at)
                return place

            return lax.fori_loop(0, sy // 16, part, carry)

        lax.fori_loop(0, sx // 4, quad, (jnp.int32(0), jnp.int32(0)))


def full_place(q, plane, i):
    flat = i // 8 * 32 + plane * 8 + i % 8
    return 2 * q + flat // 64, flat % 64 * 128


def trial_kernel(meta, wave_in, pot_in, out_ref, kind_ref, held, wave_ref, pot_ref, arrived):
    size = box_size(meta)
    sx, sy, sz = size
    per_dest = (sx * sy * sz) // (PEERS * 128)
    kind = jnp.int32(0)
    for volume in VOLUMES:
        kind = kind + (volume < per_dest).astype(jnp.int32)
    kind_ref[0] = kind
    quads = sx // 4

    def fetch(q):
        lanes = pl.ds(aligned(q * 4 * PLANE), 4 * PLANE)
        wave = pltpu.make_async_copy(wave_in.at[:, lanes], wave_ref.at[:, lanes], arrived.at[0, q])
        return wave, pltpu.make_async_copy(pot_in.at[:, lanes], pot_ref.at[:, lanes], arrived.at[1, q])

    def begin(q, carry):
        for copy in fetch(q):
            copy.start()
        return carry

    def ready(q):
        @pl.when(q < quads)
        def _():
            for copy in fetch(q):
                copy.wait()

    lax.fori_loop(0, quads, begin, 0)
    ready(0)
    lane = lax.broadcasted_iota(jnp.int32, (8, 128), 1)
    z = lane % BOX
    low = lane < BOX
    has_last = (z > 0).astype(f32)
    zero = jnp.zeros((8, 128), f32)

    def load(x, i):
        return wave_ref[:, pl.ds(aligned(x * PLANE + i * 128), 128)].astype(f32)

    def edges(x):
        before = jnp.where(x > 0, 1.0, 0.0)
        after = jnp.where(x + 4 < sx, 1.0, 0.0)
        return before, after, jnp.maximum(x - 1, 0), jnp.minimum(x + 4, sx - 1)

    def stencil(c, turned, last_turned, next_turned, around, has_next, x, i):
        beside = turned + jnp.where(low, last_turned, next_turned)
        beside = beside + (pltpu.roll(c, 127, 1) * has_next + pltpu.roll(c, 1, 1) * has_last)
        beside = beside + around
        pot = pot_ref[:, pl.ds(aligned(x * PLANE + i * 128), 128)]
        return c * ((1.0 - 3.0 * step_size) - step_size * pot) + (0.5 * step_size) * beside

    @pl.when(per_dest == VOLUMES[-1])
    def _():
        has_next = (z < BOX - 1).astype(f32)

        def quad(q, carry):
            ready(q + 1)
            x = 4 * q
            before, after, xb, xa = edges(x)
            last_turned, here = [zero] * 4, [load(x + p, 0) for p in range(4)]
            turned = [pltpu.roll(c, BOX, 1) for c in here]
            for i in range(32):
                ahead = [load(x + p, i + 1) for p in range(4)] if i < 31 else [zero] * 4
                ahead_turned = [pltpu.roll(c, BOX, 1) for c in ahead] if i < 31 else [zero] * 4
                line = [load(xb, i) * before] + here + [load(xa, i) * after]
                for p in range(4):
                    around = line[p] + line[p + 2]
                    value = stencil(here[p], turned[p], last_turned[p], ahead_turned[p], around, has_next, x + p, i)
                    dest, slot = full_place(q, p, i)
                    out_ref[dest, :, slot : slot + 128] = value.astype(bf16)
                here, last_turned, turned = ahead, turned, ahead_turned
            return carry

        lax.fori_loop(0, BOX // 4, quad, 0)

    def some(deep):
        live = (z < deep).astype(f32)
        has_next = (z < deep - 1).astype(f32)

        def part(x, g, at):
            before, after, xb, xa = edges(x)
            top = jnp.where(g > 0, 1.0, 0.0)
            bottom = jnp.where(16 * g + 16 < sy, 1.0, 0.0)
            first, last = jnp.maximum(8 * g - 1, 0), jnp.minimum(8 * g + 8, 31)
            lines = []
            for p in range(4):
                inner = [load(x + p, 8 * g + i) for i in range(8)]
                lines.append([load(x + p, first) * top] + inner + [load(x + p, last) * bottom])
            turned = [[pltpu.roll(c, BOX, 1) for c in line] for line in lines]
            for i in range(8):
                line = [load(xb, 8 * g + i) * before] + [lines[p][i + 1] for p in range(4)] + [load(xa, 8 * g + i) * after]
                for p in range(4):
                    t = turned[p]
                    around = line[p] + line[p + 2]
                    value = stencil(line[p + 1], t[i + 1], t[i], t[i + 2], around, has_next, x + p, 8 * g + i)
                    if deep == BOX:
                        dest, slot = at(p, i)
                        out_ref[dest, :, pl.ds(slot, 128)] = value.astype(bf16)
                    else:
                        held[:, p * 1024 + i * 128 : p * 1024 + (i + 1) * 128] = value * live
            if deep == BOX:
                return

            def kept(p, i):
                return held[:, p * 1024 + i * 128 : p * 1024 + (i + 1) * 128]

            for i in range(8):
                for p in range(deep // 16):
                    if deep == 32:
                        value = kept(2 * p, i) + pltpu.roll(kept(2 * p + 1, i), 32, 1)
                    else:
                        piece = (z >= 16 * p) & (z < 16 * p + 16)
                        value = kept(p, i) + pltpu.roll(jnp.where(piece, kept(3, i), 0.0), 48 - 16 * p, 1)
                    dest, slot = at(p, i)
                    out_ref[dest, :, pl.ds(slot, 128)] = value.astype(bf16)

        each_part(size, per_dest, deep, part, ready)

    for deep in (32, 48, 64):
        some(deep)


def unpack_kernel(meta, in_ref, out_ref):
    size = box_size(meta)
    sx, sy, sz = size
    per_dest = (sx * sy * sz) // (PEERS * 128)
    lane = lax.broadcasted_iota(jnp.int32, (8, 128), 1)
    z = lane % BOX

    def put(x, i, value):
        out_ref[:, pl.ds(aligned(x * PLANE + i * 128), 128)] = value.astype(bf16)

    @pl.when(per_dest == VOLUMES[-1])
    def _():
        def quad(q, carry):
            for i in range(32):
                for p in range(4):
                    dest, slot = full_place(q, p, i)
                    put(4 * q + p, i, in_ref[dest, :, slot : slot + 128])
            return carry

        lax.fori_loop(0, BOX // 4, quad, 0)

    @pl.when(per_dest < VOLUMES[-1])
    def _():
        def clear(i, carry):
            out_ref[:, pl.ds(aligned(i * PLANE), PLANE)] = jnp.zeros((8, PLANE), bf16)
            return carry

        lax.fori_loop(0, BOX, clear, 0)

    def some(deep):
        live = (z < deep).astype(f32)
        gap = (z >= deep).astype(f32)

        def part(x, g, at):
            for i in range(8):
                row = 8 * g + i
                values = []
                for p in range(deep // 16):
                    dest, slot = at(p, i)
                    values.append(in_ref[dest, :, pl.ds(slot, 128)])
                if deep == 64:
                    for p in range(4):
                        put(x + p, row, values[p])
                    continue
                values = [value.astype(f32) for value in values]
                if deep == 32:
                    for p in range(2):
                        put(x + 2 * p, row, values[p] * live)
                        put(x + 2 * p + 1, row, pltpu.roll(values[p], 96, 1) * live)
                else:
                    for p in range(3):
                        put(x + p, row, values[p] * live)
                    rest = [pltpu.roll(values[p] * gap, 80 + 16 * p, 1) for p in range(3)]
                    put(x + 3, row, rest[0] + rest[1] + rest[2])

        each_part(size, per_dest, deep, part)

    for deep in (32, 48, 64):
        some(deep)


def gram_kernel(rows_ref, out_ref):
    total = jnp.zeros((NB, NB), f32)
    for i in range(OWN):
        block = rows_ref[:, i * EXTRA : (i + 1) * EXTRA]
        total = total + lax.dot_general(block, block, (((1,), (1,)), ((), ())), preferred_element_type=f32)
    out_ref[...] = total


def halves(value):
    head = value.astype(bf16)
    return head, (value - head.astype(f32)).astype(bf16)


def product(left, right):
    dot = functools.partial(jnp.dot, preferred_element_type=f32)
    return dot(left[0], right[0]) + (dot(left[0], right[1]) + dot(left[1], right[0]))


def newton_kernel(gram_ref, out_ref):
    gram = gram_ref[...] * (1.0 / CELLS)
    frobenius = jnp.sqrt(jnp.sum(gram * gram, keepdims=True) + epsilon)
    row = lax.broadcasted_iota(jnp.int32, (NB, NB), 0)
    column = lax.broadcasted_iota(jnp.int32, (NB, NB), 1)
    three = jnp.where(row == column, 1.5, 0.0)
    square = gram / frobenius
    step = halves(three - 0.5 * square)
    inverse = step
    square = halves(product(halves(square), step))
    for sweep in range(1, NS_ITERS):
        step = halves(three - 0.5 * product(inverse, square))
        if sweep < NS_ITERS - 1:
            square = halves(product(square, step))
        inverse = product(step, inverse)
        if sweep < NS_ITERS - 1:
            inverse = halves(inverse)
    out_ref[...] = (inverse / jnp.sqrt(frobenius)).T.astype(bf16)


def fresh_kernel(coeff_ref, rows_ref, occ_ref, out_ref, dens):
    weight = jnp.broadcast_to(occ_ref[...] * (1.0 / NB), (128, NB)).T[:, 0:1]
    coeff = coeff_ref[...]
    for i in range(OWN):
        fresh = jnp.dot(coeff, rows_ref[:, i * EXTRA : (i + 1) * EXTRA], preferred_element_type=f32)
        out_ref[:, i * EXTRA : (i + 1) * EXTRA] = fresh.astype(bf16)
        sums = jnp.sum(weight * fresh * fresh, axis=0, keepdims=True)
        for j in range(8):
            dens[j : j + 1, i * 128 : (i + 1) * 128] = sums[:, j * 128 : (j + 1) * 128]
    block = dens[...].astype(bf16)
    for peer in range(PEERS):
        out_ref[peer * OWN : (peer + 1) * OWN, FULL:] = block


def share_kernel(meta, dens_ref, table_ref, out_ref, box):
    sx, sy, sz = box_size(meta)
    frag, band = meta[PLACE, 0], meta[PLACE, 1]
    groups = sy // 16
    lane = lax.broadcasted_iota(jnp.int32, (8, 128), 1)
    z = lane % BOX
    live = (z < sz).astype(f32)

    @pl.when(sx * sy * sz < CELLS)
    def _():
        box[...] = jnp.zeros((BOX, 32, 128), f32)

    def tile(at):
        return dens_ref[at // 8, :, pl.ds(aligned(at % 8 * 128), 128)].astype(f32)

    def put(x, g, value):
        box[x, pl.ds(pl.multiple_of(g * 8, 8), 8), :] = value

    def parts(deep, body):
        @pl.when(sz == deep)
        def _():
            def outer(q, carry):
                def inner(g, c):
                    body(4 * q, g, [tile((q * groups + g) * (deep // 16) + p) for p in range(deep // 16)])
                    return c

                return lax.fori_loop(0, groups, inner, carry)

            lax.fori_loop(0, sx // 4, outer, 0)

    def whole(x, g, values):
        for p in range(4):
            put(x + p, g, values[p])

    def half(x, g, values):
        for p in range(2):
            put(x + 2 * p, g, values[p] * live)
            put(x + 2 * p + 1, g, pltpu.roll(values[p], 96, 1) * live)

    def most(x, g, values):
        gap = (z >= 48).astype(f32)
        for p in range(3):
            put(x + p, g, values[p] * live)
        rest = [pltpu.roll(values[p] * gap, 80 + 16 * p, 1) for p in range(3)]
        put(x + 3, g, rest[0] + rest[1] + rest[2])

    parts(64, whole)
    parts(32, half)
    parts(48, most)

    ox, oy, _ = box_offset(meta, frag)

    def plane(x):
        inside = ((x >= 0) & (x < sx)).astype(f32)
        return (box[jnp.clip(x, 0, BOX - 1)] * inside).astype(bf16)

    for i in range(4):
        value = plane(4 * band + i - ox)
        for other in range(8):
            out_ref[other, i * 32 : (i + 1) * 32, :] = value
    for other in range(8):
        for j in range(2):
            value = plane(box_offset(meta, other)[0] + 2 * band + j - ox)
            out_ref[other, (4 + j) * 32 : (5 + j) * 32, :] = value

    wide = lax.broadcasted_iota(jnp.int32, (32, 128), 1)
    even = table_ref[pl.ds(oy, 32, stride=2), :]
    odd = table_ref[pl.ds(oy + 1, 32, stride=2), :]
    weights = []
    for k in range(4):
        pick = wide == 4 * band + k
        first = jnp.sum(jnp.where(pick, even, 0.0), axis=1, keepdims=True)
        second = jnp.sum(jnp.where(pick, odd, 0.0), axis=1, keepdims=True)
        weights.append(jnp.where(wide < BOX, first, second))
    low = lane < BOX
    for pair in range(2):
        for part in range(4):
            rows = []
            for half in range(2):
                start = part * 16 + half * 8
                cube = box[start : start + 8]
                sums = []
                for k in (2 * pair, 2 * pair + 1):
                    s = jnp.sum(cube * weights[k][None], axis=1)
                    sums.append(s + pltpu.roll(s, BOX, 1))
                rows.append(jnp.where(low, sums[0], sums[1]))
            value = jnp.concatenate(rows, axis=0).astype(bf16)
            at = 192 + pair * BOX + part * 16
            for other in range(8):
                out_ref[other, at : at + 16, :] = value


def place_kernel(meta, in_ref, patched_ref, placed, target):
    lane = lax.broadcasted_iota(jnp.int32, (32, 128), 1)
    low = lane < BOX
    wide = lax.broadcasted_iota(jnp.int32, (BOX, G), 1)
    line = lax.broadcasted_iota(jnp.int32, (BOX, G), 0)
    for f in range(8):
        _, oy, oz = box_offset(meta, f)
        sign = meta[SIGNS, f].astype(f32)
        for i in range(6):
            value = in_ref[f, i * 32 : (i + 1) * 32, :].astype(f32)
            first = pltpu.roll(jnp.where(low, value, 0.0), oz, 1)
            second = pltpu.roll(jnp.where(low, 0.0, value), (oz + BOX) % G, 1)
            placed[f * BOX : f * BOX + 32, i * G : (i + 1) * G] = first.astype(bf16)
            placed[f * BOX + 32 : (f + 1) * BOX, i * G : (i + 1) * G] = second.astype(bf16)
        lands = oy + 2 * (line % 32) + line // 32
        target[f * BOX : (f + 1) * BOX, :] = jnp.where(wide == lands, sign, 0.0).astype(bf16)
    across = (((0,), (0,)), ((), ()))
    patched_ref[...] = lax.dot_general(target[...], placed[...], across, preferred_element_type=f32)


def solve_kernel(meta, in_ref, table_ref, column_ref, row_ref, out_ref, spread, along, cols, turned):
    frag, band = meta[PLACE, 0], meta[PLACE, 1]
    dot = functools.partial(lax.dot_general, preferred_element_type=f32)
    across = (((0,), (0,)), ((), ()))
    half = lax.broadcasted_iota(jnp.int32, (G, G), 1) < BOX
    for f in range(8):
        ox, _, oz = box_offset(meta, f)
        sign = meta[SIGNS, f].astype(f32)
        part = table_ref[pl.ds(oz, BOX), :]
        part = halves(jnp.concatenate([part, part], axis=0))
        value = in_ref[f, 192:320, :].astype(f32)
        both = jnp.concatenate([jnp.where(half, value, 0.0), jnp.where(half, 0.0, value)], axis=0).astype(bf16)
        both = jnp.dot(both, part[0], preferred_element_type=f32) + jnp.dot(both, part[1], preferred_element_type=f32)
        for parity in range(2):
            for pair in range(2):
                k = 2 * pair + parity
                at = parity * G + pair * BOX
                spread[f * BOX : (f + 1) * BOX, k * G : (k + 1) * G] = both[at : at + BOX, :]
        along[f * BOX : (f + 1) * BOX, :] = table_ref[pl.ds(ox, BOX), :] * sign
    left, right = halves(along[...]), halves(spread[...])
    spectrum = dot(left[0], right[0], across) + (dot(left[0], right[1], across) + dot(left[1], right[0], across))
    table = halves(table_ref[0:G, :])
    ex = column_ref[...]
    ez = row_ref[...]
    spot = lax.broadcasted_iota(jnp.int32, (1, G), 1)
    scaled = []
    for k in range(4):
        ey = jnp.sum(jnp.where(spot == 4 * band + k, ez, 0.0), axis=1, keepdims=True)
        scaled.append(spectrum[:, k * G : (k + 1) * G] * (screening / (ex + ey + ez + screening)))
    solved = product(table, halves(jnp.concatenate(scaled, axis=1)))
    for k in range(4):
        cols[k, 0:G, :] = product(halves(solved[:, k * G : (k + 1) * G]), table)
        cols[k, G : G + BOX, :] = jnp.zeros((BOX, G), f32)
    ox = box_offset(meta, frag)[0]
    for k in range(4):
        for i in range(6):
            part = cols[k, pl.ds(i, 32, stride=4), :] if i < 4 else cols[k, pl.ds(ox + i - 4, 32, stride=2), :]
            turned[i % 3, pl.ds(2 * k + i // 3, 32, stride=8), :] = part
    for i in range(3):
        out_ref[:, i * G : (i + 1) * G] = turned[i].astype(bf16)


def total_kernel(meta, in_ref, local_ref, table_ref, slab_ref, window_ref, columns, rows):
    sx, sy, sz = box_size(meta)
    frag, band = meta[PLACE, 0], meta[PLACE, 1]
    _, oy, oz = box_offset(meta, frag)
    table = halves(table_ref[0:G, :])
    for i in range(3):
        columns[i] = in_ref[:, i * G : (i + 1) * G].astype(f32)

    def total(i):
        part = columns[i % 3, pl.ds(i // 3, G, stride=2), :].astype(bf16)
        hartree = jnp.dot(table[0], part, preferred_element_type=f32) + jnp.dot(table[1], part, preferred_element_type=f32)
        return hartree - local_ref[:, i * G : (i + 1) * G]

    for i in range(4):
        slab_ref[i] = total(i)
    lane = lax.broadcasted_iota(jnp.int32, (32, 128), 1)
    line = lax.broadcasted_iota(jnp.int32, (32, 128), 0)
    live = ((lane % BOX < sz) & (2 * line + lane // BOX < sy)).astype(f32)
    low = lane < BOX
    for j in range(2):
        rows[0:G, :] = total(4 + j)
        rows[G : G + BOX, :] = jnp.zeros((BOX, G), f32)
        even = pltpu.roll(rows[pl.ds(oy, 32, stride=2), :], (G - oz) % G, 1)
        odd = pltpu.roll(rows[pl.ds(oy + 1, 32, stride=2), :], (G + BOX - oz) % G, 1)
        inside = (2 * band + j < sx).astype(f32)
        value = (jnp.where(low, even, odd) * live * inside).astype(bf16)
        for peer in range(PEERS):
            window_ref[peer, j * 32 : (j + 1) * 32, :] = value


def swap(block, axis="band"):
    return lax.all_to_all(block, axis, split_axis=0, concat_axis=0, tiled=True)


def swap_trial(volume, trial):
    lanes = volume * 128
    if lanes == FULL:
        return swap(trial)
    return jnp.pad(swap(trial[:, :, :lanes]), ((0, 0), (0, 0), (0, FULL - lanes)))


def swap_fresh(volume, block):
    lanes = volume * 128
    if lanes == FULL:
        return swap(block)
    tiles = -(-volume // OWN)
    width = tiles * 128
    back = swap(jnp.concatenate([block[:, :, :lanes], block[:, :, FULL : FULL + width]], axis=2))
    dens = back[:, :, lanes:].reshape(PEERS, OWN, tiles, 128).transpose(0, 2, 1, 3).reshape(PEERS, OWN * width)
    dens = jnp.pad(dens[:, :lanes].reshape(PEERS * lanes), (0, CELLS - PEERS * lanes))
    dens = dens.reshape(PEERS, OWN, OWN, 128).transpose(0, 2, 1, 3).reshape(PEERS, OWN, EXTRA)
    return jnp.concatenate([jnp.pad(back[:, :, :lanes], ((0, 0), (0, 0), (0, FULL - lanes))), dens], axis=2)


def body(wave_coeffs, old_potential, occupations, box_sizes, box_offsets, patch_signs):
    fragment = lax.axis_index("frag")
    band_index = lax.axis_index("band")
    here = jnp.where(jnp.arange(8) == 0, fragment, band_index).astype(jnp.int32)
    meta = jnp.concatenate([box_sizes.T, box_offsets.T, patch_signs[None], here[None]], axis=0)
    padded, eigen = sine_table()
    table = jnp.asarray(padded)
    eigen_row, eigen_column = jnp.asarray(eigen[None, :]), jnp.asarray(eigen[:, None])

    trial, kind = pl.pallas_call(
        trial_kernel,
        out_shape=(jax.ShapeDtypeStruct((PEERS, OWN, FULL), bf16), jax.ShapeDtypeStruct((1,), jnp.int32)),
        in_specs=[smem(), pl.BlockSpec(memory_space=pltpu.HBM), pl.BlockSpec(memory_space=pltpu.HBM)],
        out_specs=(vmem(), smem()),
        scratch_shapes=[
            pltpu.VMEM((OWN, 4096), f32),
            pltpu.VMEM((OWN, CELLS), bf16),
            pltpu.VMEM((1, CELLS), f32),
            pltpu.SemaphoreType.DMA((2, BOX // 4)),
        ],
        compiler_params=params(53),
        name="trial",
    )(meta, wave_coeffs[0], old_potential)
    kind = kind[0]
    rows = lax.switch(kind, [functools.partial(swap_trial, v) for v in VOLUMES], trial)
    rows = rows.reshape(NB, FULL)
    partial_value = pl.pallas_call(
        gram_kernel,
        out_shape=jax.ShapeDtypeStruct((NB, NB), f32),
        in_specs=[vmem()],
        out_specs=vmem(),
        compiler_params=params(16),
        name="gram",
    )(rows)
    share = swap(partial_value.reshape(PEERS, OWN, NB)).sum(axis=0)
    gram = swap(jnp.broadcast_to(share[None], (PEERS, OWN, NB))).reshape(NB, NB)
    coeff = pl.pallas_call(
        newton_kernel,
        out_shape=jax.ShapeDtypeStruct((NB, NB), bf16),
        in_specs=[vmem()],
        out_specs=vmem(),
        compiler_params=params(16),
        name="newton",
    )(gram)
    fresh = pl.pallas_call(
        fresh_kernel,
        out_shape=jax.ShapeDtypeStruct((NB, FULL + EXTRA), bf16),
        in_specs=[vmem(), vmem(), vmem()],
        out_specs=vmem(),
        scratch_shapes=[pltpu.VMEM((OWN, EXTRA), f32)],
        compiler_params=params(16),
        name="fresh",
    )(coeff, rows, occupations)
    fresh = fresh.reshape(PEERS, OWN, FULL + EXTRA)
    back = lax.switch(kind, [functools.partial(swap_fresh, v) for v in VOLUMES], fresh)
    shared = pl.pallas_call(
        share_kernel,
        out_shape=jax.ShapeDtypeStruct((8, 320, 128), bf16),
        grid=(1,),
        in_specs=[
            smem(),
            pl.BlockSpec((PEERS, OWN, EXTRA), lambda i: (0, 0, FULL // EXTRA)),
            pl.BlockSpec((G + BOX, G), lambda i: (0, 0)),
        ],
        out_specs=pl.BlockSpec((8, 320, 128), lambda i: (0, 0, 0)),
        scratch_shapes=[pltpu.VMEM((BOX, 32, 128), f32)],
        compiler_params=params(32),
        name="share",
    )(meta, back, table)
    parts = swap(shared, "frag")
    columns = pl.pallas_call(
        solve_kernel,
        out_shape=jax.ShapeDtypeStruct((2 * G, 3 * G), bf16),
        in_specs=[smem(), vmem(), vmem(), vmem(), vmem()],
        out_specs=vmem(),
        scratch_shapes=[
            pltpu.VMEM((8 * BOX, 4 * G), f32),
            pltpu.VMEM((8 * BOX, G), f32),
            pltpu.VMEM((4, G + BOX, G), f32),
            pltpu.VMEM((3, 2 * G, G), f32),
        ],
        compiler_params=params(32),
        name="solve",
    )(meta, parts, table, eigen_column, eigen_row)
    patched = pl.pallas_call(
        place_kernel,
        out_shape=jax.ShapeDtypeStruct((G, 6 * G), f32),
        in_specs=[smem(), vmem()],
        out_specs=vmem(),
        scratch_shapes=[pltpu.VMEM((8 * BOX, 6 * G), bf16), pltpu.VMEM((8 * BOX, G), bf16)],
        compiler_params=params(32),
        cost_estimate=pl.CostEstimate(flops=2 * 8 * BOX * 6 * G * G, bytes_accessed=2**20, transcendentals=0),
        name="place",
    )(meta, parts)
    columns = swap(columns.reshape(PEERS, 8, 3 * G)).reshape(2 * G, 3 * G)
    local = local_factor * jnp.cbrt(jnp.maximum(patched, 0.0))
    total_potential, window = pl.pallas_call(
        total_kernel,
        out_shape=(jax.ShapeDtypeStruct((4, G, G), f32), jax.ShapeDtypeStruct((PEERS, 64, 128), bf16)),
        in_specs=[smem(), vmem(), vmem(), vmem()],
        out_specs=(vmem(), vmem()),
        scratch_shapes=[pltpu.VMEM((3, 2 * G, G), f32), pltpu.VMEM((G + BOX, G), f32)],
        compiler_params=params(32),
        name="total",
    )(meta, columns, local, table)
    window = swap(window)
    waves_out = pl.pallas_call(
        unpack_kernel,
        out_shape=jax.ShapeDtypeStruct((OWN, CELLS), bf16),
        in_specs=[smem(), vmem()],
        out_specs=vmem(),
        compiler_params=params(32),
        name="unpack",
    )(meta, back)
    box_potential = window.astype(f32).reshape(1, CELLS)
    return (waves_out[None], box_potential, total_potential)


def solution(mesh):
    placed = (P("frag", "band", None), P("frag", None), P("frag", None), P(), P(), P())
    return jax.shard_map(
        body,
        mesh=mesh,
        in_specs=placed,
        out_specs=(P("frag", "band", None), P("frag", None), P("band", None, None)),
        check_vma=False,
    )
```

```python
import functools

import jax
import jax.numpy as jnp
import numpy as np
from jax import lax
from jax.experimental import pallas as pl
from jax.experimental.pallas import tpu as pltpu
from jax.sharding import PartitionSpec as P

NB = 256
BOX = 64
G = 128
NS_ITERS = 8
CELLS = BOX**3
PLANE = BOX * BOX
PEERS = 32
OWN = NB // PEERS
FULL = CELLS // PEERS
EXTRA = FULL // OWN
SIZES, OFFSETS, SIGNS, PLACE = 0, 3, 6, 7
VOLUMES = (8, 12, 16, 18, 24, 27, 32, 36, 48, 64)

step_size = 0.1
screening = 0.5
local_factor = 0.75
epsilon = 1e-06
f32 = jnp.float32
bf16 = jnp.bfloat16


def sine_table():
    index = np.arange(G, dtype=np.float64) + 1.0
    table = np.sqrt(2.0 / (G + 1)) * np.sin(np.pi * index[:, None] * index[None, :] / (G + 1))
    eigen = 2.0 - 2.0 * np.cos(np.pi * index / (G + 1))
    padded = np.zeros((G + BOX, G), np.float32)
    padded[:G] = table
    return padded, eigen.astype(np.float32)


def aligned(offset):
    return pl.multiple_of(offset, 128)


def vmem():
    return pl.BlockSpec(memory_space=pltpu.VMEM)


def smem():
    return pl.BlockSpec(memory_space=pltpu.SMEM)


def box_size(meta):
    f = meta[PLACE, 0]
    return meta[SIZES, f], meta[SIZES + 1, f], meta[SIZES + 2, f]


def box_offset(meta, f):
    return meta[OFFSETS, f], meta[OFFSETS + 1, f], meta[OFFSETS + 2, f]


def params(mib):
    return pltpu.CompilerParams(vmem_limit_bytes=mib * 1024 * 1024)


def runs(total, run, per_dest, carry):
    dest, slot = carry
    places = []
    for _ in range(total // run):
        places.append((dest, slot))
        slot = slot + run
        wrap = slot == per_dest
        dest, slot = jnp.where(wrap, dest + 1, dest), jnp.where(wrap, 0, slot)
    return places, (dest, slot)


def each_part(size, per_dest, deep, body, ready=None):
    sx, sy, sz = size
    run = {64: 4, 32: 2, 48: 1}[deep]

    @pl.when((sz == deep) & (per_dest < VOLUMES[-1]))
    def _():
        def quad(q, carry):
            if ready is not None:
                ready(q + 1)

            def part(g, place):
                places, place = runs(deep // 2, run, per_dest, place)

                def at(plane, i):
                    dest, slot = places[(plane * 8 + i) // run]
                    return dest, aligned((slot + i % run) * 128)

                body(4 * q, g, at)
                return place

            return lax.fori_loop(0, sy // 16, part, carry)

        lax.fori_loop(0, sx // 4, quad, (jnp.int32(0), jnp.int32(0)))


def full_place(q, plane, i):
    flat = i // 8 * 32 + plane * 8 + i % 8
    return 2 * q + flat // 64, flat % 64 * 128


def trial_kernel(meta, wave_in, pot_in, out_ref, kind_ref, held, wave_ref, pot_ref, arrived):
    size = box_size(meta)
    sx, sy, sz = size
    per_dest = (sx * sy * sz) // (PEERS * 128)
    kind = jnp.int32(0)
    for volume in VOLUMES:
        kind = kind + (volume < per_dest).astype(jnp.int32)
    kind_ref[0] = kind
    quads = sx // 4

    def fetch(q):
        lanes = pl.ds(aligned(q * 4 * PLANE), 4 * PLANE)
        wave = pltpu.make_async_copy(wave_in.at[:, lanes], wave_ref.at[:, lanes], arrived.at[0, q])
        return wave, pltpu.make_async_copy(pot_in.at[:, lanes], pot_ref.at[:, lanes], arrived.at[1, q])

    def begin(q, carry):
        for copy in fetch(q):
            copy.start()
        return carry

    def ready(q):
        @pl.when(q < quads)
        def _():
            for copy in fetch(q):
                copy.wait()

        @pl.when(q + 4 < quads)
        def _():
            begin(q + 4, 0)

    lax.fori_loop(0, 4, begin, 0)
    ready(0)
    lane = lax.broadcasted_iota(jnp.int32, (8, 128), 1)
    z = lane % BOX
    low = lane < BOX
    has_last = (z > 0).astype(f32)
    zero = jnp.zeros((8, 128), f32)

    def load(x, i):
        return wave_ref[:, pl.ds(aligned(x * PLANE + i * 128), 128)].astype(f32)

    def edges(x):
        before = jnp.where(x > 0, 1.0, 0.0)
        after = jnp.where(x + 4 < sx, 1.0, 0.0)
        return before, after, jnp.maximum(x - 1, 0), jnp.minimum(x + 4, sx - 1)

    def stencil(c, turned, last_turned, next_turned, around, has_next, x, i):
        beside = turned + jnp.where(low, last_turned, next_turned)
        beside = beside + (pltpu.roll(c, 127, 1) * has_next + pltpu.roll(c, 1, 1) * has_last)
        beside = beside + around
        pot = pot_ref[:, pl.ds(aligned(x * PLANE + i * 128), 128)]
        return c * ((1.0 - 3.0 * step_size) - step_size * pot) + (0.5 * step_size) * beside

    @pl.when(per_dest == VOLUMES[-1])
    def _():
        has_next = (z < BOX - 1).astype(f32)

        def quad(q, carry):
            ready(q + 1)
            x = 4 * q
            before, after, xb, xa = edges(x)
            last_turned, here = [zero] * 4, [load(x + p, 0) for p in range(4)]
            turned = [pltpu.roll(c, BOX, 1) for c in here]
            for i in range(32):
                ahead = [load(x + p, i + 1) for p in range(4)] if i < 31 else [zero] * 4
                ahead_turned = [pltpu.roll(c, BOX, 1) for c in ahead] if i < 31 else [zero] * 4
                line = [load(xb, i) * before] + here + [load(xa, i) * after]
                for p in range(4):
                    around = line[p] + line[p + 2]
                    value = stencil(here[p], turned[p], last_turned[p], ahead_turned[p], around, has_next, x + p, i)
                    dest, slot = full_place(q, p, i)
                    out_ref[dest, :, slot : slot + 128] = value.astype(bf16)
                here, last_turned, turned = ahead, turned, ahead_turned
            return carry

        lax.fori_loop(0, BOX // 4, quad, 0)

    def some(deep):
        live = (z < deep).astype(f32)
        has_next = (z < deep - 1).astype(f32)

        def part(x, g, at):
            before, after, xb, xa = edges(x)
            top = jnp.where(g > 0, 1.0, 0.0)
            bottom = jnp.where(16 * g + 16 < sy, 1.0, 0.0)
            first, last = jnp.maximum(8 * g - 1, 0), jnp.minimum(8 * g + 8, 31)
            lines = []
            for p in range(4):
                inner = [load(x + p, 8 * g + i) for i in range(8)]
                lines.append([load(x + p, first) * top] + inner + [load(x + p, last) * bottom])
            turned = [[pltpu.roll(c, BOX, 1) for c in line] for line in lines]
            for i in range(8):
                line = [load(xb, 8 * g + i) * before] + [lines[p][i + 1] for p in range(4)] + [load(xa, 8 * g + i) * after]
                for p in range(4):
                    t = turned[p]
                    around = line[p] + line[p + 2]
                    value = stencil(line[p + 1], t[i + 1], t[i], t[i + 2], around, has_next, x + p, 8 * g + i)
                    if deep == BOX:
                        dest, slot = at(p, i)
                        out_ref[dest, :, pl.ds(slot, 128)] = value.astype(bf16)
                    else:
                        held[:, p * 1024 + i * 128 : p * 1024 + (i + 1) * 128] = value * live
            if deep == BOX:
                return

            def kept(p, i):
                return held[:, p * 1024 + i * 128 : p * 1024 + (i + 1) * 128]

            for i in range(8):
                for p in range(deep // 16):
                    if deep == 32:
                        value = kept(2 * p, i) + pltpu.roll(kept(2 * p + 1, i), 32, 1)
                    else:
                        piece = (z >= 16 * p) & (z < 16 * p + 16)
                        value = kept(p, i) + pltpu.roll(jnp.where(piece, kept(3, i), 0.0), 48 - 16 * p, 1)
                    dest, slot = at(p, i)
                    out_ref[dest, :, pl.ds(slot, 128)] = value.astype(bf16)

        each_part(size, per_dest, deep, part, ready)

    for deep in (32, 48, 64):
        some(deep)


def unpack_kernel(meta, in_ref, out_ref):
    size = box_size(meta)
    sx, sy, sz = size
    per_dest = (sx * sy * sz) // (PEERS * 128)
    lane = lax.broadcasted_iota(jnp.int32, (8, 128), 1)
    z = lane % BOX

    def put(x, i, value):
        out_ref[:, pl.ds(aligned(x * PLANE + i * 128), 128)] = value.astype(bf16)

    @pl.when(per_dest == VOLUMES[-1])
    def _():
        def quad(q, carry):
            for i in range(32):
                for p in range(4):
                    dest, slot = full_place(q, p, i)
                    put(4 * q + p, i, in_ref[dest, :, slot : slot + 128])
            return carry

        lax.fori_loop(0, BOX // 4, quad, 0)

    @pl.when(per_dest < VOLUMES[-1])
    def _():
        def clear(i, carry):
            out_ref[:, pl.ds(aligned(i * PLANE), PLANE)] = jnp.zeros((8, PLANE), bf16)
            return carry

        lax.fori_loop(0, BOX, clear, 0)

    def some(deep):
        live = (z < deep).astype(f32)
        gap = (z >= deep).astype(f32)

        def part(x, g, at):
            for i in range(8):
                row = 8 * g + i
                values = []
                for p in range(deep // 16):
                    dest, slot = at(p, i)
                    values.append(in_ref[dest, :, pl.ds(slot, 128)])
                if deep == 64:
                    for p in range(4):
                        put(x + p, row, values[p])
                    continue
                values = [value.astype(f32) for value in values]
                if deep == 32:
                    for p in range(2):
                        put(x + 2 * p, row, values[p] * live)
                        put(x + 2 * p + 1, row, pltpu.roll(values[p], 96, 1) * live)
                else:
                    for p in range(3):
                        put(x + p, row, values[p] * live)
                    rest = [pltpu.roll(values[p] * gap, 80 + 16 * p, 1) for p in range(3)]
                    put(x + 3, row, rest[0] + rest[1] + rest[2])

        each_part(size, per_dest, deep, part)

    for deep in (32, 48, 64):
        some(deep)


def gram_kernel(rows_ref, out_ref):
    total = jnp.zeros((NB, NB), f32)
    for i in range(OWN):
        block = rows_ref[:, i * EXTRA : (i + 1) * EXTRA]
        total = total + lax.dot_general(block, block, (((1,), (1,)), ((), ())), preferred_element_type=f32)
    out_ref[...] = total


def halves(value):
    head = value.astype(bf16)
    return head, (value - head.astype(f32)).astype(bf16)


def product(left, right):
    dot = functools.partial(jnp.dot, preferred_element_type=f32)
    return dot(left[0], right[0]) + (dot(left[0], right[1]) + dot(left[1], right[0]))


def newton_kernel(gram_ref, out_ref):
    gram = gram_ref[...] * (1.0 / CELLS)
    frobenius = jnp.sqrt(jnp.sum(gram * gram, keepdims=True) + epsilon)
    row = lax.broadcasted_iota(jnp.int32, (NB, NB), 0)
    column = lax.broadcasted_iota(jnp.int32, (NB, NB), 1)
    three = jnp.where(row == column, 1.5, 0.0)
    square = gram / frobenius
    step = halves(three - 0.5 * square)
    inverse = step
    square = halves(product(halves(square), step))
    for sweep in range(1, NS_ITERS):
        step = halves(three - 0.5 * product(inverse, square))
        if sweep < NS_ITERS - 1:
            square = halves(product(square, step))
        inverse = product(step, inverse)
        if sweep < NS_ITERS - 1:
            inverse = halves(inverse)
    out_ref[...] = (inverse / jnp.sqrt(frobenius)).T.astype(bf16)


def fresh_kernel(coeff_ref, rows_ref, occ_ref, out_ref, dens):
    weight = jnp.broadcast_to(occ_ref[...] * (1.0 / NB), (128, NB)).T[:, 0:1]
    coeff = coeff_ref[...]
    for i in range(OWN):
        fresh = jnp.dot(coeff, rows_ref[:, i * EXTRA : (i + 1) * EXTRA], preferred_element_type=f32)
        out_ref[:, i * EXTRA : (i + 1) * EXTRA] = fresh.astype(bf16)
        sums = jnp.sum(weight * fresh * fresh, axis=0, keepdims=True)
        for j in range(8):
            dens[j : j + 1, i * 128 : (i + 1) * 128] = sums[:, j * 128 : (j + 1) * 128]
    block = dens[...].astype(bf16)
    for peer in range(PEERS):
        out_ref[peer * OWN : (peer + 1) * OWN, FULL:] = block


def share_kernel(meta, dens_ref, table_ref, out_ref, box):
    sx, sy, sz = box_size(meta)
    frag, band = meta[PLACE, 0], meta[PLACE, 1]
    groups = sy // 16
    lane = lax.broadcasted_iota(jnp.int32, (8, 128), 1)
    z = lane % BOX
    live = (z < sz).astype(f32)

    @pl.when(sx * sy * sz < CELLS)
    def _():
        box[...] = jnp.zeros((BOX, 32, 128), f32)

    def tile(at):
        return dens_ref[at // 8, :, pl.ds(aligned(at % 8 * 128), 128)].astype(f32)

    def put(x, g, value):
        box[x, pl.ds(pl.multiple_of(g * 8, 8), 8), :] = value

    def parts(deep, body):
        @pl.when(sz == deep)
        def _():
            def outer(q, carry):
                def inner(g, c):
                    body(4 * q, g, [tile((q * groups + g) * (deep // 16) + p) for p in range(deep // 16)])
                    return c

                return lax.fori_loop(0, groups, inner, carry)

            lax.fori_loop(0, sx // 4, outer, 0)

    def whole(x, g, values):
        for p in range(4):
            put(x + p, g, values[p])

    def half(x, g, values):
        for p in range(2):
            put(x + 2 * p, g, values[p] * live)
            put(x + 2 * p + 1, g, pltpu.roll(values[p], 96, 1) * live)

    def most(x, g, values):
        gap = (z >= 48).astype(f32)
        for p in range(3):
            put(x + p, g, values[p] * live)
        rest = [pltpu.roll(values[p] * gap, 80 + 16 * p, 1) for p in range(3)]
        put(x + 3, g, rest[0] + rest[1] + rest[2])

    parts(64, whole)
    parts(32, half)
    parts(48, most)

    ox, oy, _ = box_offset(meta, frag)

    def plane(x):
        inside = ((x >= 0) & (x < sx)).astype(f32)
        return (box[jnp.clip(x, 0, BOX - 1)] * inside).astype(bf16)

    for i in range(4):
        value = plane(4 * band + i - ox)
        for other in range(8):
            out_ref[other, i * 32 : (i + 1) * 32, :] = value
    for other in range(8):
        for j in range(2):
            value = plane(box_offset(meta, other)[0] + 2 * band + j - ox)
            out_ref[other, (4 + j) * 32 : (5 + j) * 32, :] = value

    wide = lax.broadcasted_iota(jnp.int32, (32, 128), 1)
    even = table_ref[pl.ds(oy, 32, stride=2), :]
    odd = table_ref[pl.ds(oy + 1, 32, stride=2), :]
    weights = []
    for k in range(4):
        pick = wide == 4 * band + k
        first = jnp.sum(jnp.where(pick, even, 0.0), axis=1, keepdims=True)
        second = jnp.sum(jnp.where(pick, odd, 0.0), axis=1, keepdims=True)
        weights.append(jnp.where(wide < BOX, first, second))
    low = lane < BOX
    for pair in range(2):
        for part in range(4):
            rows = []
            for half in range(2):
                start = part * 16 + half * 8
                cube = box[start : start + 8]
                sums = []
                for k in (2 * pair, 2 * pair + 1):
                    s = jnp.sum(cube * weights[k][None], axis=1)
                    sums.append(s + pltpu.roll(s, BOX, 1))
                rows.append(jnp.where(low, sums[0], sums[1]))
            value = jnp.concatenate(rows, axis=0).astype(bf16)
            at = 192 + pair * BOX + part * 16
            for other in range(8):
                out_ref[other, at : at + 16, :] = value


def place_kernel(meta, in_ref, patched_ref, placed, target):
    lane = lax.broadcasted_iota(jnp.int32, (32, 128), 1)
    low = lane < BOX
    wide = lax.broadcasted_iota(jnp.int32, (BOX, G), 1)
    line = lax.broadcasted_iota(jnp.int32, (BOX, G), 0)
    for f in range(8):
        _, oy, oz = box_offset(meta, f)
        sign = meta[SIGNS, f].astype(f32)
        for i in range(6):
            value = in_ref[f, i * 32 : (i + 1) * 32, :].astype(f32)
            first = pltpu.roll(jnp.where(low, value, 0.0), oz, 1)
            second = pltpu.roll(jnp.where(low, 0.0, value), (oz + BOX) % G, 1)
            placed[f * BOX : f * BOX + 32, i * G : (i + 1) * G] = first.astype(bf16)
            placed[f * BOX + 32 : (f + 1) * BOX, i * G : (i + 1) * G] = second.astype(bf16)
        lands = oy + 2 * (line % 32) + line // 32
        target[f * BOX : (f + 1) * BOX, :] = jnp.where(wide == lands, sign, 0.0).astype(bf16)
    across = (((0,), (0,)), ((), ()))
    patched_ref[...] = lax.dot_general(target[...], placed[...], across, preferred_element_type=f32)


def solve_kernel(meta, in_ref, table_ref, column_ref, row_ref, out_ref, spread, along, cols, turned):
    frag, band = meta[PLACE, 0], meta[PLACE, 1]
    dot = functools.partial(lax.dot_general, preferred_element_type=f32)
    across = (((0,), (0,)), ((), ()))
    half = lax.broadcasted_iota(jnp.int32, (G, G), 1) < BOX
    for f in range(8):
        ox, _, oz = box_offset(meta, f)
        sign = meta[SIGNS, f].astype(f32)
        part = table_ref[pl.ds(oz, BOX), :]
        part = halves(jnp.concatenate([part, part], axis=0))
        value = in_ref[f, 192:320, :].astype(f32)
        both = jnp.concatenate([jnp.where(half, value, 0.0), jnp.where(half, 0.0, value)], axis=0).astype(bf16)
        both = jnp.dot(both, part[0], preferred_element_type=f32) + jnp.dot(both, part[1], preferred_element_type=f32)
        for parity in range(2):
            for pair in range(2):
                k = 2 * pair + parity
                at = parity * G + pair * BOX
                spread[f * BOX : (f + 1) * BOX, k * G : (k + 1) * G] = both[at : at + BOX, :]
        along[f * BOX : (f + 1) * BOX, :] = table_ref[pl.ds(ox, BOX), :] * sign
    left, right = halves(along[...]), halves(spread[...])
    spectrum = dot(left[0], right[0], across) + (dot(left[0], right[1], across) + dot(left[1], right[0], across))
    table = halves(table_ref[0:G, :])
    ex = column_ref[...]
    ez = row_ref[...]
    spot = lax.broadcasted_iota(jnp.int32, (1, G), 1)
    scaled = []
    for k in range(4):
        ey = jnp.sum(jnp.where(spot == 4 * band + k, ez, 0.0), axis=1, keepdims=True)
        scaled.append(spectrum[:, k * G : (k + 1) * G] * (screening / (ex + ey + ez + screening)))
    solved = product(table, halves(jnp.concatenate(scaled, axis=1)))
    for k in range(4):
        cols[k, 0:G, :] = product(halves(solved[:, k * G : (k + 1) * G]), table)
        cols[k, G : G + BOX, :] = jnp.zeros((BOX, G), f32)
    ox = box_offset(meta, frag)[0]
    for k in range(4):
        for i in range(6):
            part = cols[k, pl.ds(i, 32, stride=4), :] if i < 4 else cols[k, pl.ds(ox + i - 4, 32, stride=2), :]
            turned[i % 3, pl.ds(2 * k + i // 3, 32, stride=8), :] = part
    for i in range(3):
        out_ref[:, i * G : (i + 1) * G] = turned[i].astype(bf16)


def total_kernel(meta, in_ref, local_ref, table_ref, slab_ref, window_ref, columns, rows):
    sx, sy, sz = box_size(meta)
    frag, band = meta[PLACE, 0], meta[PLACE, 1]
    _, oy, oz = box_offset(meta, frag)
    table = halves(table_ref[0:G, :])
    for i in range(3):
        columns[i] = in_ref[:, i * G : (i + 1) * G].astype(f32)

    def total(i):
        part = columns[i % 3, pl.ds(i // 3, G, stride=2), :].astype(bf16)
        hartree = jnp.dot(table[0], part, preferred_element_type=f32) + jnp.dot(table[1], part, preferred_element_type=f32)
        return hartree - local_ref[:, i * G : (i + 1) * G]

    for i in range(4):
        slab_ref[i] = total(i)
    lane = lax.broadcasted_iota(jnp.int32, (32, 128), 1)
    line = lax.broadcasted_iota(jnp.int32, (32, 128), 0)
    live = ((lane % BOX < sz) & (2 * line + lane // BOX < sy)).astype(f32)
    low = lane < BOX
    for j in range(2):
        rows[0:G, :] = total(4 + j)
        rows[G : G + BOX, :] = jnp.zeros((BOX, G), f32)
        even = pltpu.roll(rows[pl.ds(oy, 32, stride=2), :], (G - oz) % G, 1)
        odd = pltpu.roll(rows[pl.ds(oy + 1, 32, stride=2), :], (G + BOX - oz) % G, 1)
        inside = (2 * band + j < sx).astype(f32)
        value = (jnp.where(low, even, odd) * live * inside).astype(bf16)
        for peer in range(PEERS):
            window_ref[peer, j * 32 : (j + 1) * 32, :] = value


def swap(block, axis="band"):
    return lax.all_to_all(block, axis, split_axis=0, concat_axis=0, tiled=True)


def swap_trial(volume, trial):
    lanes = volume * 128
    if lanes == FULL:
        return swap(trial)
    return jnp.pad(swap(trial[:, :, :lanes]), ((0, 0), (0, 0), (0, FULL - lanes)))


def swap_fresh(volume, block):
    lanes = volume * 128
    if lanes == FULL:
        return swap(block)
    tiles = -(-volume // OWN)
    width = tiles * 128
    back = swap(jnp.concatenate([block[:, :, :lanes], block[:, :, FULL : FULL + width]], axis=2))
    dens = back[:, :, lanes:].reshape(PEERS, OWN, tiles, 128).transpose(0, 2, 1, 3).reshape(PEERS, OWN * width)
    dens = jnp.pad(dens[:, :lanes].reshape(PEERS * lanes), (0, CELLS - PEERS * lanes))
    dens = dens.reshape(PEERS, OWN, OWN, 128).transpose(0, 2, 1, 3).reshape(PEERS, OWN, EXTRA)
    return jnp.concatenate([jnp.pad(back[:, :, :lanes], ((0, 0), (0, 0), (0, FULL - lanes))), dens], axis=2)


def body(wave_coeffs, old_potential, occupations, box_sizes, box_offsets, patch_signs):
    fragment = lax.axis_index("frag")
    band_index = lax.axis_index("band")
    here = jnp.where(jnp.arange(8) == 0, fragment, band_index).astype(jnp.int32)
    meta = jnp.concatenate([box_sizes.T, box_offsets.T, patch_signs[None], here[None]], axis=0)
    padded, eigen = sine_table()
    table = jnp.asarray(padded)
    eigen_row, eigen_column = jnp.asarray(eigen[None, :]), jnp.asarray(eigen[:, None])

    trial, kind = pl.pallas_call(
        trial_kernel,
        out_shape=(jax.ShapeDtypeStruct((PEERS, OWN, FULL), bf16), jax.ShapeDtypeStruct((1,), jnp.int32)),
        in_specs=[smem(), pl.BlockSpec(memory_space=pltpu.HBM), pl.BlockSpec(memory_space=pltpu.HBM)],
        out_specs=(vmem(), smem()),
        scratch_shapes=[
            pltpu.VMEM((OWN, 4096), f32),
            pltpu.VMEM((OWN, CELLS), bf16),
            pltpu.VMEM((1, CELLS), f32),
            pltpu.SemaphoreType.DMA((2, BOX // 4)),
        ],
        compiler_params=params(53),
        name="trial",
    )(meta, wave_coeffs[0], old_potential)
    kind = kind[0]
    rows = lax.switch(kind, [functools.partial(swap_trial, v) for v in VOLUMES], trial)
    rows = rows.reshape(NB, FULL)
    partial_value = pl.pallas_call(
        gram_kernel,
        out_shape=jax.ShapeDtypeStruct((NB, NB), f32),
        in_specs=[vmem()],
        out_specs=vmem(),
        compiler_params=params(16),
        name="gram",
    )(rows)
    share = swap(partial_value.reshape(PEERS, OWN, NB)).sum(axis=0)
    gram = swap(jnp.broadcast_to(share[None], (PEERS, OWN, NB))).reshape(NB, NB)
    coeff = pl.pallas_call(
        newton_kernel,
        out_shape=jax.ShapeDtypeStruct((NB, NB), bf16),
        in_specs=[vmem()],
        out_specs=vmem(),
        compiler_params=params(16),
        name="newton",
    )(gram)
    fresh = pl.pallas_call(
        fresh_kernel,
        out_shape=jax.ShapeDtypeStruct((NB, FULL + EXTRA), bf16),
        in_specs=[vmem(), vmem(), vmem()],
        out_specs=vmem(),
        scratch_shapes=[pltpu.VMEM((OWN, EXTRA), f32)],
        compiler_params=params(16),
        name="fresh",
    )(coeff, rows, occupations)
    fresh = fresh.reshape(PEERS, OWN, FULL + EXTRA)
    back = lax.switch(kind, [functools.partial(swap_fresh, v) for v in VOLUMES], fresh)
    shared = pl.pallas_call(
        share_kernel,
        out_shape=jax.ShapeDtypeStruct((8, 320, 128), bf16),
        grid=(1,),
        in_specs=[
            smem(),
            pl.BlockSpec((PEERS, OWN, EXTRA), lambda i: (0, 0, FULL // EXTRA)),
            pl.BlockSpec((G + BOX, G), lambda i: (0, 0)),
        ],
        out_specs=pl.BlockSpec((8, 320, 128), lambda i: (0, 0, 0)),
        scratch_shapes=[pltpu.VMEM((BOX, 32, 128), f32)],
        compiler_params=params(32),
        name="share",
    )(meta, back, table)
    parts = swap(shared, "frag")
    columns = pl.pallas_call(
        solve_kernel,
        out_shape=jax.ShapeDtypeStruct((2 * G, 3 * G), bf16),
        in_specs=[smem(), vmem(), vmem(), vmem(), vmem()],
        out_specs=vmem(),
        scratch_shapes=[
            pltpu.VMEM((8 * BOX, 4 * G), f32),
            pltpu.VMEM((8 * BOX, G), f32),
            pltpu.VMEM((4, G + BOX, G), f32),
            pltpu.VMEM((3, 2 * G, G), f32),
        ],
        compiler_params=params(32),
        name="solve",
    )(meta, parts, table, eigen_column, eigen_row)
    patched = pl.pallas_call(
        place_kernel,
        out_shape=jax.ShapeDtypeStruct((G, 6 * G), f32),
        in_specs=[smem(), vmem()],
        out_specs=vmem(),
        scratch_shapes=[pltpu.VMEM((8 * BOX, 6 * G), bf16), pltpu.VMEM((8 * BOX, G), bf16)],
        compiler_params=params(32),
        cost_estimate=pl.CostEstimate(flops=2 * 8 * BOX * 6 * G * G, bytes_accessed=2**20, transcendentals=0),
        name="place",
    )(meta, parts)
    columns = swap(columns.reshape(PEERS, 8, 3 * G)).reshape(2 * G, 3 * G)
    local = local_factor * jnp.cbrt(jnp.maximum(patched, 0.0))
    total_potential, window = pl.pallas_call(
        total_kernel,
        out_shape=(jax.ShapeDtypeStruct((4, G, G), f32), jax.ShapeDtypeStruct((PEERS, 64, 128), bf16)),
        in_specs=[smem(), vmem(), vmem(), vmem()],
        out_specs=(vmem(), vmem()),
        scratch_shapes=[pltpu.VMEM((3, 2 * G, G), f32), pltpu.VMEM((G + BOX, G), f32)],
        compiler_params=params(32),
        name="total",
    )(meta, columns, local, table)
    window = swap(window)
    waves_out = pl.pallas_call(
        unpack_kernel,
        out_shape=jax.ShapeDtypeStruct((OWN, CELLS), bf16),
        in_specs=[smem(), vmem()],
        out_specs=vmem(),
        compiler_params=params(32),
        name="unpack",
    )(meta, back)
    box_potential = window.astype(f32).reshape(1, CELLS)
    return (waves_out[None], box_potential, total_potential)


def solution(mesh):
    placed = (P("frag", "band", None), P("frag", None), P("frag", None), P(), P(), P())
    return jax.shard_map(
        body,
        mesh=mesh,
        in_specs=placed,
        out_specs=(P("frag", "band", None), P("frag", None), P("band", None, None)),
        check_vma=False,
    )
```
